1024 devices in a mesh: node: 64 (over x, z), local: 16 (over y, core).
Axes of the slice: x: 4, y: 8, z: 16, core: 2. Of those that a mesh axis runs over, the one named last changes fastest.
Arguments:
- tokens: bfloat16 [8192, 3584], P('node', 'local'), may hold values from -6 to 6
- cotangent: bfloat16 [8192, 3584], P('node', 'local'), may hold values from -6 to 6
- routes: int32 [8192, 8], P('node'), may hold values from 0 to 255, as said below
- gate_probs: bfloat16 [8192, 8], P('node'), may hold values from 0.049804688 to 0.5
- w_gate: bfloat16 [64, 3584, 2048], P('node', None, 'local'), may hold values from -0.09375 to 0.09375
- w_up: bfloat16 [64, 3584, 2048], P('node', None, 'local'), may hold values from -0.09375 to 0.09375
- w_down: bfloat16 [64, 2048, 3584], P('node', 'local'), may hold values from -0.125 to 0.125
- tile_noise: float32 [64, 3, 28, 2048], P('node', None, None, 'local'), may hold values from -0.5 to 0.5
Outputs:
- token_grad: bfloat16 [8192, 3584], P('node', 'local')
- probs_grad: bfloat16 [8192, 8], P('node')
- noise_grad: float32 [64, 3, 28, 2048], P('node', None, None, 'local')
The draws below stay inside these ranges and needn't reach their ends.
Inputs may be any that keep to these rules, and one draw needn't show every extreme that they name: `routes`: each token names 8 different experts, two in each of 4 different groups, expert e lying in group e // 4. Among the 128 tokens of one index of node at most 2 name a given group's first expert (index a multiple of 4); in every draw one group's first expert is named by exactly 2 of them at every index of node.
All inputs are finite; a program needn't handle non-finite values.
Results may differ from the reference program's by a relative error of at most 0.029.
Values may be sent and summed in bfloat16 or wider, within the bound.
No kernel may reach another device: no remote copies, remote signals or barrier semaphores. Data moves between devices by JAX's collectives and lax.ppermute only.
A program may use at most 32 MiB of HBM per device.

```python
import jax
import jax.numpy as jnp
from jax import lax

D = 3584
H = 2048
EXP_GROUP = 4
TOPK = 8
GROUP_LIMIT = 4
TOK_GROUP = 128
TOKENS = 8192
FLIGHT = 64
DBLK = 28
ARRIVE = 8
CAP = 2
N_NODE = 64
N_LOCAL = 16


def draw_routes(key, part):
    key = jax.random.fold_in(key, 11)
    subkeys = jax.random.split(key, 6)
    orders = jax.vmap(lambda subkey: jax.random.permutation(subkey, N_NODE))(jax.random.split(subkeys[0], N_NODE))
    full_group = jax.random.randint(subkeys[1], (), 0, N_NODE)
    least = max(1, CAP // 3)
    fills = jax.random.randint(subkeys[2], (N_NODE, N_NODE), least, CAP + 1)
    fills = jnp.where(jnp.arange(N_NODE)[None, :] == full_group, CAP, fills)
    shifts = jax.random.randint(subkeys[3], (N_NODE, N_NODE), 0, ARRIVE)
    positions = jnp.arange(TOK_GROUP)
    group_slot = jnp.arange(GROUP_LIMIT)
    cycle_pos = GROUP_LIMIT * positions[:, None] + group_slot[None, :]
    residue = cycle_pos % N_NODE
    cycle_rank = cycle_pos // N_NODE
    group_ids = orders[:, residue]
    flat_groups = group_ids.reshape(N_NODE, -1)
    fill_here = jnp.take_along_axis(fills, flat_groups, axis=1).reshape(group_ids.shape)
    shift_here = jnp.take_along_axis(shifts, flat_groups, axis=1).reshape(group_ids.shape)
    takes_first = (cycle_rank[None, :, :] + shift_here) % ARRIVE < fill_here
    partner = jax.random.randint(subkeys[4], group_ids.shape, 1, EXP_GROUP)
    dropped = jax.random.randint(subkeys[5], group_ids.shape, 1, EXP_GROUP)
    lower_pick = jnp.where(dropped == 1, 2, 1)
    upper_pick = jnp.where(dropped == 3, 2, 3)
    pick_one = jnp.where(takes_first, 0, lower_pick)
    pick_two = jnp.where(takes_first, partner, upper_pick)
    expert_ids = group_ids[..., None] * EXP_GROUP + jnp.stack([pick_one, pick_two], axis=-1)
    return expert_ids.reshape(TOKENS, TOPK).astype(jnp.int32)


def level_of(own_key, extent, shards, low, top_value):
    factor_of = 1.0
    for position, blocks in shards:
        draws = jax.random.uniform(jax.random.fold_in(jax.random.fold_in(own_key, 6), position), (blocks,), jnp.float32, low / len(shards), top_value / len(shards))
        factor_of = factor_of * jnp.repeat(jnp.exp(draws), extent[position] // blocks).reshape((-1,) + (1,) * (len(extent) - 1 - position))
    return factor_of


def gaussian(rng, shape, spread, bound, cuts=(), held_as=jnp.bfloat16):
    level = level_of(rng, shape, cuts, -0.22, 0.18) if cuts else 1.0
    result = jax.random.normal(rng, shape, jnp.float32) * spread * level
    return jnp.minimum(jnp.maximum(result, -bound), bound).astype(held_as)


def setup_inputs(seed: int = 0) -> dict:
    key_list = jax.random.split(jax.random.key(seed), 9)
    return {
        "tokens": gaussian(key_list[0], (TOKENS, D), 1.0, 6.0, ((0, 64), (1, 16))),
        "cotangent": gaussian(key_list[1], (TOKENS, D), 1.0, 6.0, ((0, 64), (1, 16))),
        "routes": draw_routes(jax.random.fold_in(key_list[8], 71), 0),
        "gate_probs": jnp.clip(0.049804688 + 0.4501953 * jax.random.uniform(key_list[3], (TOKENS, TOPK), jnp.float32) ** level_of(key_list[3], (TOKENS, TOPK), ((0, 64),), -0.2, 0.2), 0.049804688, 0.5).astype(jnp.bfloat16),
        "w_gate": gaussian(key_list[4], (FLIGHT, D, H), D ** -0.5, 0.09375, ((0, 64), (2, 16))),
        "w_up": gaussian(key_list[5], (FLIGHT, D, H), D ** -0.5, 0.09375, ((0, 64), (2, 16))),
        "w_down": gaussian(key_list[6], (FLIGHT, H, D), H ** -0.5, 0.125, ((0, 64), (1, 16))),
        "tile_noise": jnp.clip(jax.random.uniform(key_list[7], (FLIGHT, 3, DBLK, H), jnp.float32, -0.5, 0.5) * level_of(key_list[7], (FLIGHT, 3, DBLK, H), ((0, 64), (3, 16)), -0.4, 0.0), -0.5, 0.5),
    }


def scale_gate(weight, rates):
    feat_width, hid_width = weight.shape
    blocks = rates.shape[0]
    scaled = weight.astype(jnp.float32).reshape(blocks, feat_width // blocks, hid_width) * (1.0 + rates[:, None, :])
    return scaled.reshape(feat_width, hid_width).astype(jnp.bfloat16)


def scale_down(weight, rates):
    hid_width, feat_width = weight.shape
    blocks = rates.shape[0]
    scaled = weight.astype(jnp.float32).reshape(hid_width, blocks, feat_width // blocks) * (1.0 + rates.T[:, :, None])
    return scaled.reshape(hid_width, feat_width).astype(jnp.bfloat16)


def tiles_gate(weight, grad, blocks):
    feat_width, hid_width = weight.shape
    return jnp.sum((weight.astype(jnp.float32) * grad).reshape(blocks, feat_width // blocks, hid_width), axis=1)


def tiles_down(weight, grad, blocks):
    hid_width, feat_width = weight.shape
    return jnp.sum((weight.astype(jnp.float32) * grad).reshape(hid_width, blocks, feat_width // blocks), axis=2).T


def expert_pass(rows_x, rows_dy, probs_col, gate_k, up_k, down_k, rates):
    blocks = rates.shape[1]
    eff_gate = scale_gate(gate_k, rates[0])
    eff_up = scale_gate(up_k, rates[1])
    eff_down = scale_down(down_k, rates[2])
    pre_gate = jnp.dot(rows_x, eff_gate, preferred_element_type=jnp.float32)
    pre_up = jnp.dot(rows_x, eff_up, preferred_element_type=jnp.float32)
    sigmoid_gate = jax.nn.sigmoid(pre_gate)
    swish_gate = pre_gate * sigmoid_gate
    hidden = (swish_gate * pre_up).astype(jnp.bfloat16)
    back_hidden = jnp.dot(rows_dy, eff_down.T, preferred_element_type=jnp.float32)
    grad_hidden = probs_col * back_hidden
    d_gate_pre = (grad_hidden * pre_up * sigmoid_gate * (1.0 + pre_gate * (1.0 - sigmoid_gate))).astype(jnp.bfloat16)
    d_up_pre = (grad_hidden * swish_gate).astype(jnp.bfloat16)
    scaled = (probs_col * hidden.astype(jnp.float32)).astype(jnp.bfloat16)
    grad_down = jnp.dot(scaled.T, rows_dy, preferred_element_type=jnp.float32)
    grad_gate = jnp.dot(rows_x.T, d_gate_pre, preferred_element_type=jnp.float32)
    grad_up = jnp.dot(rows_x.T, d_up_pre, preferred_element_type=jnp.float32)
    noise_grad = jnp.stack([tiles_gate(gate_k, grad_gate, blocks), tiles_gate(up_k, grad_up, blocks), tiles_down(down_k, grad_down, blocks)])
    row_count = rows_x.shape[0]
    feat_width, hid_width = eff_gate.shape
    part = hid_width // N_LOCAL
    gate_parts = d_gate_pre.astype(jnp.float32).reshape(row_count, N_LOCAL, part)
    up_parts = d_up_pre.astype(jnp.float32).reshape(row_count, N_LOCAL, part)
    gate_cols = eff_gate.astype(jnp.float32).reshape(feat_width, N_LOCAL, part)
    up_cols = eff_up.astype(jnp.float32).reshape(feat_width, N_LOCAL, part)
    terms = jnp.einsum("snh,dnh->nsd", gate_parts, gate_cols) + jnp.einsum("snh,dnh->nsd", up_parts, up_cols)
    rounded = lax.optimization_barrier(terms.astype(jnp.bfloat16))
    expert_dx = jnp.sum(rounded.astype(jnp.float32), axis=0).astype(jnp.bfloat16)
    prob_parts = jnp.sum((hidden.astype(jnp.float32) * back_hidden).reshape(row_count, N_LOCAL, part), axis=2)
    prob_round = lax.optimization_barrier(prob_parts.astype(jnp.bfloat16))
    expert_prob = jnp.sum(prob_round.astype(jnp.float32), axis=1).astype(jnp.bfloat16)
    return expert_dx, expert_prob, noise_grad


def reference(tokens, cotangent, routes, gate_probs, w_gate, w_up, w_down, tile_noise):
    group_rows = TOK_GROUP
    firsts = jnp.arange(N_NODE, dtype=jnp.int32) * EXP_GROUP
    matched = (routes[:, :, None] == firsts[None, None, :]).astype(jnp.float32)
    hit_flag = jnp.sum(matched, axis=1).astype(jnp.int32)
    weight_tk = jnp.sum(gate_probs.astype(jnp.float32)[:, :, None] * matched, axis=1)
    hit_blocks = hit_flag.reshape(N_NODE, group_rows, N_NODE)
    slot_rank = jnp.cumsum(hit_blocks, axis=1) - hit_blocks
    slot_ids = jnp.arange(CAP, dtype=jnp.int32)
    slot_hit = (hit_blocks[..., None] == 1) & (slot_rank[..., None] == slot_ids[None, None, None, :])
    live = jnp.any(slot_hit, axis=1)
    positions = jnp.arange(group_rows, dtype=jnp.int32)
    local_index = jnp.sum(jnp.where(slot_hit, positions[None, :, None, None], 0), axis=1).astype(jnp.int32)
    token_index = local_index + (jnp.arange(N_NODE, dtype=jnp.int32) * group_rows)[:, None, None]
    rows_all = jnp.transpose(token_index, (1, 0, 2)).reshape(N_NODE, N_NODE * CAP)
    live_all = jnp.transpose(live, (1, 0, 2)).reshape(N_NODE, N_NODE * CAP)

    def per_expert(items):
        gate_k, up_k, down_k, rates, rows, valid, expert = items
        rows_x = jnp.where(valid[:, None], tokens[rows], jnp.zeros((), jnp.bfloat16)).astype(jnp.bfloat16)
        rows_dy = jnp.where(valid[:, None], cotangent[rows], jnp.zeros((), jnp.bfloat16)).astype(jnp.bfloat16)
        probs_col = jnp.where(valid, weight_tk[rows, expert], jnp.zeros((), jnp.float32))[:, None]
        return expert_pass(rows_x, rows_dy, probs_col, gate_k, up_k, down_k, rates)

    expert_ids = jnp.arange(N_NODE, dtype=jnp.int32)
    dx_all, prob_all, noise_grad = lax.map(per_expert, (w_gate, w_up, w_down, tile_noise, rows_all, live_all, expert_ids))
    flat_rows = rows_all.reshape(-1)
    flat_live = live_all.reshape(-1)
    flat_expert = jnp.repeat(expert_ids, N_NODE * CAP)
    dx_values = jnp.where(flat_live[:, None], dx_all.reshape(-1, tokens.shape[1]).astype(jnp.float32), jnp.zeros((), jnp.float32))
    token_grad = jnp.zeros(tokens.shape, jnp.float32).at[flat_rows].add(dx_values).astype(jnp.bfloat16)
    prob_values = jnp.where(flat_live, prob_all.reshape(-1).astype(jnp.float32), jnp.zeros((), jnp.float32))
    per_group = jnp.zeros((tokens.shape[0], N_NODE), jnp.float32).at[flat_rows, flat_expert].add(prob_values)
    probs_grad = jnp.einsum("tjk,tk->tj", matched, per_group).astype(jnp.bfloat16)
    return token_grad, probs_grad, noise_grad
```

```python
import jax
import jax.numpy as jnp
from jax import lax
from jax.experimental import pallas as pl
from jax.experimental.pallas import tpu as pltpu
from jax.sharding import PartitionSpec as P

EXP_GROUP = 4
LANES = 128
F32 = jnp.float32
BF16 = jnp.bfloat16
ROWS_BY_ROWS = (((0,), (0,)), ((), ()))
LANES_BY_LANES = (((1,), (1,)), ((), ()))


def dot(a, b, dims=(((1,), (0,)), ((), ()))):
    return lax.dot_general(a, b, dims, preferred_element_type=F32)


def select_rows(routes_ref, per_group, copies, rows):
    top, tokens = routes_ref.shape
    row = lax.broadcasted_iota(jnp.int32, (rows, tokens), 0)
    first = lax.div(row, per_group) * EXP_GROUP
    slot = lax.rem(lax.div(row, copies), per_group // copies)
    matches = [routes_ref[j : j + 1, :] == first for j in range(top)]
    hit = jnp.zeros((rows, tokens), F32)
    for match in matches:
        hit = jnp.where(match, 1.0, hit)
    before = lax.broadcasted_iota(jnp.int32, (tokens, tokens), 0)
    after = lax.broadcasted_iota(jnp.int32, (tokens, tokens), 1)
    earlier = jnp.where(before < after, 1.0, 0.0).astype(BF16)
    rank = dot(hit.astype(BF16), earlier)
    chosen = jnp.where(rank == slot.astype(F32), hit, 0.0)
    return chosen, lax.rem(row, copies), matches


def pack_kernel(routes_ref, probs_ref, x_ref, dy_ref, out_ref):
    rows, lanes = out_ref.shape
    feats = x_ref.shape[0]
    chosen, block, matches = select_rows(routes_ref, 8, 4, rows)
    weight = jnp.zeros(chosen.shape, F32)
    for j, match in enumerate(matches):
        weight = jnp.where(match, probs_ref[j : j + 1, :].astype(F32), weight)
    weight = jnp.sum(weight * chosen, axis=1, keepdims=True)
    pad = jnp.zeros((4 * lanes - 2 * feats, lanes), BF16)
    both = jnp.concatenate([x_ref[...], dy_ref[...], pad], axis=0)
    picked = dot(chosen.astype(BF16), both, LANES_BY_LANES)
    out = jnp.zeros((rows, lanes), F32)
    for j in range(4):
        out = jnp.where(block == j, picked[:, j * lanes : (j + 1) * lanes], out)
    lane = lax.broadcasted_iota(jnp.int32, (rows, lanes), 1)
    out = jnp.where((block == 3) & (lane == 2 * feats - 3 * lanes), weight, out)
    out_ref[...] = out.astype(BF16)


def unpack_kernel(got_ref, xdy_ref, prob_ref):
    rows, lanes = got_ref.shape
    got = got_ref[...]
    row = lax.broadcasted_iota(jnp.int32, (rows, lanes), 0)
    col = lax.broadcasted_iota(jnp.int32, (rows, lanes), 1)
    for j in range(4):
        place = jnp.where(row == 4 * col + j, 1.0, 0.0).astype(BF16)
        part = dot(got, place, ROWS_BY_ROWS)
        if j < 3:
            xdy_ref[j * lanes : (j + 1) * lanes, :] = part.astype(BF16)
        else:
            last = xdy_ref.shape[0] - 3 * lanes
            xdy_ref[3 * lanes :, :] = part[:last].astype(BF16)
            prob_ref[...] = part[last : last + 8]


def scale_kernel(gate_ref, up_ref, down_ref, noise_ref, wide_ref, tall_ref, eff_down_ref, down_t_ref):
    blocks, lanes = noise_ref.shape[1:]
    pad = jnp.zeros((lanes - blocks, lanes), F32)
    down_rates = jnp.concatenate([noise_ref[2], pad], axis=0).T
    for b in range(blocks):
        part = slice(b * lanes, (b + 1) * lanes)
        gate = (gate_ref[part, :].astype(F32) * (1.0 + noise_ref[0, b : b + 1, :])).astype(BF16)
        up = (up_ref[part, :].astype(F32) * (1.0 + noise_ref[1, b : b + 1, :])).astype(BF16)
        tall_ref[part, :lanes] = gate
        tall_ref[part, lanes:] = up
        wide_ref[:lanes, part] = gate.T
        wide_ref[lanes:, part] = up.T
        down = down_ref[:, part]
        eff_down_ref[:, part] = (down.astype(F32) * (1.0 + down_rates[:, b : b + 1])).astype(BF16)
        down_t_ref[part, :] = down.T


def gather_rows(core, mine_ref, other_ref, x_ref, dy_ref):
    chips, both, _ = mine_ref.shape
    feats = both // 2
    for chip in range(chips):
        for source, rank in ((mine_ref, core), (other_ref, 1 - core)):
            start = pl.multiple_of((2 * chip + rank) * feats, 32)
            x_ref[pl.ds(start, feats), :] = source[chip, :feats, :]
            dy_ref[pl.ds(start, feats), :] = source[chip, feats:, :]


def main_kernel(
    core_ref, mine_ref, other_ref, prob_ref, wide_ref, tall_ref, down_ref,
    keep_ref, send_ref, d_ref, x_ref, dy_ref,
):
    core = core_ref[0]
    gather_rows(core, mine_ref, other_ref, x_ref, dy_ref)
    hid = down_ref.shape[0]
    pre = dot(wide_ref[...], x_ref[...])
    pre_gate, pre_up = pre[:hid], pre[hid:]
    back = dot(down_ref[...], dy_ref[...])
    prob = prob_ref[0:1, :]
    sig = jax.nn.sigmoid(pre_gate)
    swish = pre_gate * sig
    hidden = (swish * pre_up).astype(BF16).astype(F32)
    grad_hidden = prob * back
    d_gate = grad_hidden * pre_up * sig * (1.0 + pre_gate * (1.0 - sig))
    d_up = grad_hidden * swish
    scaled = prob * hidden
    d_ref[:, :hid] = d_gate.T.astype(BF16)
    d_ref[:, hid : 2 * hid] = d_up.T.astype(BF16)
    d_ref[:, 2 * hid :] = scaled.T.astype(BF16)
    d_both = jnp.concatenate([d_gate.astype(BF16), d_up.astype(BF16)], axis=0)
    prob_term = jnp.sum(hidden * back, axis=0, keepdims=True)
    chips, rows, lanes = keep_ref.shape
    feats = x_ref.shape[0] // (2 * chips)
    line = lax.broadcasted_iota(jnp.int32, (rows - feats, lanes), 0)
    tail = jnp.where(line == 0, prob_term, 0.0).astype(BF16)
    for chip in range(chips):
        for target, rank in ((keep_ref, core), (send_ref, 1 - core)):
            start = pl.multiple_of((2 * chip + rank) * feats, 32)
            target[chip, :feats, :] = dot(tall_ref[pl.ds(start, feats), :], d_both).astype(BF16)
            target[chip, feats:, :] = tail


def noise_kernel(x_ref, dy_ref, d_ref, gate_ref, up_ref, down_t_ref, out_ref):
    blocks, lanes = out_ref.shape[1:]
    for b in range(blocks):
        part = slice(b * lanes, (b + 1) * lanes)
        grad = dot(x_ref[part, :], d_ref[:, : 2 * lanes])
        grad_down = dot(dy_ref[part, :], d_ref[:, 2 * lanes :])
        pieces = (
            (gate_ref, grad[:, :lanes]),
            (up_ref, grad[:, lanes:]),
            (down_t_ref, grad_down),
        )
        for i, (weight, value) in enumerate(pieces):
            out_ref[i, b : b + 1, :] = jnp.sum(
                weight[part, :].astype(F32) * value, axis=0, keepdims=True
            )


def collect_kernel(parts_ref, out_ref):
    rows, lanes = out_ref.shape
    chips, height, slots = parts_ref.shape
    total = parts_ref[0].astype(F32)
    for chip in range(1, chips):
        total = total + parts_ref[chip].astype(F32)
    pad = jnp.zeros((2 * lanes - height, slots), BF16)
    total = jnp.concatenate([total.astype(BF16), pad], axis=0)
    row = lax.broadcasted_iota(jnp.int32, (rows, slots), 0)
    col = lax.broadcasted_iota(jnp.int32, (rows, slots), 1)
    place = jnp.where(lax.div(row, 2) == col, 1.0, 0.0).astype(BF16)
    spread = dot(place, total, LANES_BY_LANES)
    odd = lax.rem(lax.broadcasted_iota(jnp.int32, (rows, lanes), 0), 2)
    out_ref[...] = jnp.where(odd == 0, spread[:, :lanes], spread[:, lanes:]).astype(BF16)


def finish_kernel(back_ref, routes_ref, tokens_ref, probs_ref):
    rows, lanes = back_ref.shape
    feats = tokens_ref.shape[0]
    chosen, block, matches = select_rows(routes_ref, 4, 2, rows)
    back = back_ref[...]
    low = dot(back, jnp.where(block == 0, chosen, 0.0).astype(BF16), ROWS_BY_ROWS)
    high_rows = jnp.where(block == 1, chosen, 0.0)
    high = dot(back, high_rows.astype(BF16), ROWS_BY_ROWS)
    tokens_ref[:lanes, :] = low.astype(BF16)
    tokens_ref[lanes:, :] = high[: feats - lanes].astype(BF16)
    given = back[:, feats - lanes : feats - lanes + 1].astype(F32) * high_rows
    lines = [
        jnp.sum(jnp.where(match, given, 0.0), axis=0, keepdims=True) for match in matches
    ]
    probs_ref[...] = jnp.concatenate(lines, axis=0).astype(BF16)


def call(kernel, outs, *args, scalars=0, flops=0):
    size = sum(a.size * a.dtype.itemsize for a in args) + sum(
        o.size * o.dtype.itemsize for o in outs
    )
    specs = [pl.BlockSpec(memory_space=pltpu.SMEM)] * scalars
    specs += [pl.BlockSpec(memory_space=pltpu.VMEM)] * (len(args) - scalars)
    return pl.pallas_call(
        kernel,
        out_shape=outs,
        in_specs=specs,
        out_specs=[pl.BlockSpec(memory_space=pltpu.VMEM)] * len(outs),
        compiler_params=pltpu.CompilerParams(vmem_limit_bytes=32 * 1024 * 1024),
        cost_estimate=pl.CostEstimate(flops=flops, bytes_accessed=size, transcendentals=0),
    )(*args)


def shape(dims, dtype=BF16):
    return jax.ShapeDtypeStruct(dims, dtype)


def shards(tokens, cotangent, routes, gate_probs, w_gate, w_up, w_down, tile_noise):
    nodes = lax.axis_size("node")
    local = lax.axis_size("local")
    chips = local // 2
    count, feats = tokens.shape
    slots = 2 * nodes
    gate, up, down, noise = w_gate[0], w_up[0], w_down[0], tile_noise[0]
    width, hid = gate.shape
    routes_t = routes.T
    same_core = [[2 * y + c for y in range(chips)] for c in range(2)]
    swap = [(i, i ^ 1) for i in range(local)]
    core = lax.rem(lax.axis_index("local"), 2).astype(jnp.int32).reshape(1)

    (sent,) = call(
        pack_kernel, [shape((8 * nodes, LANES))], routes_t, gate_probs.T, tokens.T, cotangent.T
    )
    got = lax.all_to_all(sent.reshape(nodes, 8, LANES), "node", 0, 0, tiled=True)
    wide, tall, eff_down, down_t = call(
        scale_kernel,
        [shape((2 * hid, width)), shape((width, 2 * hid)), shape((hid, width)), shape((width, hid))],
        gate, up, down, noise,
    )
    xdy, prob = call(
        unpack_kernel,
        [shape((2 * feats, slots)), shape((8, slots), F32)],
        got.reshape(8 * nodes, LANES),
    )
    mine = lax.all_gather(xdy, "local", axis=0, axis_index_groups=same_core)
    other = lax.ppermute(mine, "local", swap)
    rows = feats + 16
    keep, send, d_all, x_all, dy_all = call(
        main_kernel,
        [
            shape((chips, rows, slots)),
            shape((chips, rows, slots)),
            shape((slots, 3 * hid)),
            shape((width, slots)),
            shape((width, slots)),
        ],
        core, mine, other, prob, wide, tall, eff_down,
        scalars=1,
    )
    came = lax.ppermute(send, "local", swap)
    pair = (keep.astype(F32) + came.astype(F32)).astype(BF16)
    parts = lax.all_to_all(pair, "local", 0, 0, axis_index_groups=same_core, tiled=True)
    (noise_grad,) = call(
        noise_kernel, [shape(noise.shape, F32)], x_all, dy_all, d_all, gate, up, down_t
    )
    (home,) = call(collect_kernel, [shape((4 * nodes, LANES))], parts)
    back = lax.all_to_all(home.reshape(nodes, 4, LANES), "node", 0, 0, tiled=True)
    token_t, probs_t = call(
        finish_kernel,
        [shape((feats, count)), shape((routes.shape[1], count))],
        back.reshape(4 * nodes, LANES),
        routes_t,
    )
    return token_t.T, probs_t.T, noise_grad[None]


def solution(mesh):
    in_specs = (
        P("node", "local"),
        P("node", "local"),
        P("node", None),
        P("node", None),
        P("node", None, "local"),
        P("node", None, "local"),
        P("node", "local", None),
        P("node", None, None, "local"),
    )
    out_specs = (P("node", "local"), P("node", None), P("node", None, None, "local"))
    return jax.shard_map(shards, mesh=mesh, in_specs=in_specs, out_specs=out_specs, check_vma=False)
```

```python
import math

import jax
import jax.numpy as jnp
from jax import lax
from jax.experimental import pallas as pl
from jax.experimental.pallas import tpu as pltpu
from jax.sharding import PartitionSpec as P

EXP_GROUP = 4
LANES = 128
F32 = jnp.float32
BF16 = jnp.bfloat16
ROWS_BY_ROWS = (((0,), (0,)), ((), ()))
LANES_BY_LANES = (((1,), (1,)), ((), ()))


def dot(a, b, dims=(((1,), (0,)), ((), ()))):
    return lax.dot_general(a, b, dims, preferred_element_type=F32)


def select_rows(routes_ref, per_group, copies, rows):
    top, tokens = routes_ref.shape
    row = lax.broadcasted_iota(jnp.int32, (rows, tokens), 0)
    first = lax.div(row, per_group) * EXP_GROUP
    slot = lax.rem(lax.div(row, copies), per_group // copies)
    matches = [routes_ref[j : j + 1, :] == first for j in range(top)]
    hit = jnp.zeros((rows, tokens), F32)
    for match in matches:
        hit = jnp.where(match, 1.0, hit)
    before = lax.broadcasted_iota(jnp.int32, (tokens, tokens), 0)
    after = lax.broadcasted_iota(jnp.int32, (tokens, tokens), 1)
    earlier = jnp.where(before < after, 1.0, 0.0).astype(BF16)
    rank = dot(hit.astype(BF16), earlier)
    chosen = jnp.where(rank == slot.astype(F32), hit, 0.0)
    return chosen, lax.rem(row, copies), matches


def pack_kernel(routes_ref, probs_ref, x_ref, dy_ref, out_ref):
    rows, lanes = out_ref.shape
    feats = x_ref.shape[0]
    chosen, block, matches = select_rows(routes_ref, 8, 4, rows)
    weight = jnp.zeros(chosen.shape, F32)
    for j, match in enumerate(matches):
        weight = jnp.where(match, probs_ref[j : j + 1, :].astype(F32), weight)
    weight = jnp.sum(weight * chosen, axis=1, keepdims=True)
    pad = jnp.zeros((4 * lanes - 2 * feats, lanes), BF16)
    both = jnp.concatenate([x_ref[...], dy_ref[...], pad], axis=0)
    picked = dot(chosen.astype(BF16), both, LANES_BY_LANES)
    out = jnp.zeros((rows, lanes), F32)
    for j in range(4):
        out = jnp.where(block == j, picked[:, j * lanes : (j + 1) * lanes], out)
    lane = lax.broadcasted_iota(jnp.int32, (rows, lanes), 1)
    out = jnp.where((block == 3) & (lane == 2 * feats - 3 * lanes), weight, out)
    out_ref[...] = out.astype(BF16)


def unpack_kernel(got_ref, xdy_ref, prob_ref):
    rows, lanes = got_ref.shape
    got = got_ref[...]
    row = lax.broadcasted_iota(jnp.int32, (rows, lanes), 0)
    col = lax.broadcasted_iota(jnp.int32, (rows, lanes), 1)
    for j in range(4):
        place = jnp.where(row == 4 * col + j, 1.0, 0.0).astype(BF16)
        part = dot(got, place, ROWS_BY_ROWS)
        if j < 3:
            xdy_ref[j * lanes : (j + 1) * lanes, :] = part.astype(BF16)
        else:
            last = xdy_ref.shape[0] - 3 * lanes
            xdy_ref[3 * lanes :, :] = part[:last].astype(BF16)
            prob_ref[...] = part[last : last + 8]


def scale_kernel(
    core_ref, gate_ref, up_ref, down_ref, noise_ref,
    ahead_near_ref, ahead_far_ref, near_ref, far_ref, down_t_ref, both_ref, back_ref,
):
    core = core_ref[0]
    blocks, lanes = noise_ref.shape[1:]
    half = near_ref.shape[0]
    feats = half // 8
    for b in range(blocks):
        part = slice(b * lanes, (b + 1) * lanes)
        gate = gate_ref[part, :].astype(F32) * (1.0 + noise_ref[0, b : b + 1, :])
        up = up_ref[part, :].astype(F32) * (1.0 + noise_ref[1, b : b + 1, :])
        both_ref[part, :lanes] = gate.astype(BF16)
        both_ref[part, lanes : 2 * lanes] = up.astype(BF16)
        down = down_ref[:, part].T
        down_t_ref[part, :] = down
        back = down.astype(F32) * (1.0 + noise_ref[2, b : b + 1, :])
        both_ref[part, 2 * lanes :] = back.astype(BF16)
    for rank, rows_ref, ahead_ref in (
        (core, near_ref, ahead_near_ref),
        (1 - core, far_ref, ahead_far_ref),
    ):
        for chip in range(half // feats):
            part = slice(chip * feats, (chip + 1) * feats)
            rows = pl.ds(pl.multiple_of((2 * chip + rank) * feats, 32), feats)
            rows_ref[part, :] = both_ref[rows, : 2 * lanes]
            back_ref[part, :] = both_ref[rows, 2 * lanes :]
        for b in range(half // lanes):
            part = slice(b * lanes, (b + 1) * lanes)
            ahead_ref[:lanes, part] = rows_ref[part, :lanes].T
            ahead_ref[lanes : 2 * lanes, part] = rows_ref[part, lanes:].T
            ahead_ref[2 * lanes :, part] = back_ref[part, :].T


def forward(weight_ref, rows_ref):
    chips, both, _ = rows_ref.shape
    feats = both // 2
    x = jnp.concatenate([rows_ref[chip, :feats, :] for chip in range(chips)], axis=0)
    dy = jnp.concatenate([rows_ref[chip, feats:, :] for chip in range(chips)], axis=0)
    hid = weight_ref.shape[0] // 3
    pre = dot(weight_ref[: 2 * hid, :], x)
    return jnp.concatenate([pre, dot(weight_ref[2 * hid :, :], dy)], axis=0)


def first_kernel(
    mine_ref, ahead_near_ref, ahead_far_ref, near_ref, far_ref,
    part_ref, ahead_out_ref, near_out_ref, far_out_ref, rows_ref, weight_ref, sems,
):
    moves = [
        pltpu.make_async_copy(source, target, sems.at[i])
        for i, (source, target) in enumerate(
            (
                (mine_ref, rows_ref),
                (ahead_near_ref, weight_ref),
                (ahead_far_ref, ahead_out_ref),
                (near_ref, near_out_ref),
                (far_ref, far_out_ref),
            )
        )
    ]
    for move in moves:
        move.start()
    moves[0].wait()
    moves[1].wait()
    part_ref[...] = forward(weight_ref, rows_ref)
    for move in moves[2:]:
        move.wait()


def main_kernel(
    part_ref, ahead_ref, other_ref, prob_ref, near_ref, far_ref, keep_ref, send_ref, d_ref
):
    chips, rows, lanes = keep_ref.shape
    feats = near_ref.shape[0] // chips
    hid = ahead_ref.shape[0] // 3
    total = part_ref[...] + forward(ahead_ref, other_ref)
    pre_gate, pre_up, back = total[:hid], total[hid : 2 * hid], total[2 * hid :]
    prob = prob_ref[0:1, :]
    sig = jax.nn.sigmoid(pre_gate)
    swish = pre_gate * sig
    hidden = (swish * pre_up).astype(BF16).astype(F32)
    grad_hidden = prob * back
    d_gate = grad_hidden * pre_up * sig * (1.0 + pre_gate * (1.0 - sig))
    d_up = grad_hidden * swish
    d_ref[:, :hid] = d_gate.T.astype(BF16)
    d_ref[:, hid : 2 * hid] = d_up.T.astype(BF16)
    d_ref[:, 2 * hid :] = (prob * hidden).T.astype(BF16)
    d_both = jnp.concatenate([d_gate.astype(BF16), d_up.astype(BF16)], axis=0)
    prob_term = jnp.sum(hidden * back, axis=0, keepdims=True)
    line = lax.broadcasted_iota(jnp.int32, (rows - feats, lanes), 0)
    tail = jnp.where(line == 0, prob_term, 0.0).astype(BF16)
    for target, weight in ((send_ref, far_ref), (keep_ref, near_ref)):
        value = dot(weight[...], d_both).astype(BF16)
        for chip in range(chips):
            target[chip, :feats, :] = value[chip * feats : (chip + 1) * feats]
            target[chip, feats:, :] = tail


def gather_rows(core, mine_ref, other_ref, x_ref, dy_ref):
    chips, both, _ = mine_ref.shape
    feats = both // 2
    for chip in range(chips):
        for source, rank in ((mine_ref, core), (other_ref, 1 - core)):
            start = pl.multiple_of((2 * chip + rank) * feats, 32)
            x_ref[pl.ds(start, feats), :] = source[chip, :feats, :]
            dy_ref[pl.ds(start, feats), :] = source[chip, feats:, :]


def noise_kernel(
    core_ref, mine_ref, other_ref, d_ref, gate_ref, up_ref, down_t_ref, out_ref, x_ref, dy_ref
):
    gather_rows(core_ref[0], mine_ref, other_ref, x_ref, dy_ref)
    blocks, lanes = out_ref.shape[1:]
    for b in range(blocks):
        part = slice(b * lanes, (b + 1) * lanes)
        grad = dot(x_ref[part, :], d_ref[:, : 2 * lanes])
        grad_down = dot(dy_ref[part, :], d_ref[:, 2 * lanes :])
        pieces = (
            (gate_ref, grad[:, :lanes]),
            (up_ref, grad[:, lanes:]),
            (down_t_ref, grad_down),
        )
        for i, (weight, value) in enumerate(pieces):
            out_ref[i, b : b + 1, :] = jnp.sum(
                weight[part, :].astype(F32) * value, axis=0, keepdims=True
            )


def collect_kernel(parts_ref, out_ref):
    rows, lanes = out_ref.shape
    chips, height, slots = parts_ref.shape
    total = parts_ref[0].astype(F32)
    for chip in range(1, chips):
        total = total + parts_ref[chip].astype(F32)
    pad = jnp.zeros((2 * lanes - height, slots), BF16)
    total = jnp.concatenate([total.astype(BF16), pad], axis=0)
    row = lax.broadcasted_iota(jnp.int32, (rows, slots), 0)
    col = lax.broadcasted_iota(jnp.int32, (rows, slots), 1)
    place = jnp.where(lax.div(row, 2) == col, 1.0, 0.0).astype(BF16)
    spread = dot(place, total, LANES_BY_LANES)
    odd = lax.rem(lax.broadcasted_iota(jnp.int32, (rows, lanes), 0), 2)
    out_ref[...] = jnp.where(odd == 0, spread[:, :lanes], spread[:, lanes:]).astype(BF16)


def finish_kernel(back_ref, routes_ref, tokens_ref, probs_ref):
    rows, lanes = back_ref.shape
    feats = tokens_ref.shape[0]
    chosen, block, matches = select_rows(routes_ref, 4, 2, rows)
    back = back_ref[...]
    low = dot(back, jnp.where(block == 0, chosen, 0.0).astype(BF16), ROWS_BY_ROWS)
    high_rows = jnp.where(block == 1, chosen, 0.0)
    high = dot(back, high_rows.astype(BF16), ROWS_BY_ROWS)
    tokens_ref[:lanes, :] = low.astype(BF16)
    tokens_ref[lanes:, :] = high[: feats - lanes].astype(BF16)
    given = back[:, feats - lanes : feats - lanes + 1].astype(F32) * high_rows
    lines = [
        jnp.sum(jnp.where(match, given, 0.0), axis=0, keepdims=True) for match in matches
    ]
    probs_ref[...] = jnp.concatenate(lines, axis=0).astype(BF16)


def call(kernel, outs, *args, scalars=0, scratch=(), limit=32, held=pltpu.VMEM):
    size = sum(math.prod(a.shape) * a.dtype.itemsize for a in [*args, *outs])
    specs = [pl.BlockSpec(memory_space=pltpu.SMEM)] * scalars
    specs += [pl.BlockSpec(memory_space=held)] * (len(args) - scalars)
    return pl.pallas_call(
        kernel,
        out_shape=outs,
        in_specs=specs,
        out_specs=[pl.BlockSpec(memory_space=pltpu.VMEM)] * len(outs),
        scratch_shapes=list(scratch),
        compiler_params=pltpu.CompilerParams(vmem_limit_bytes=limit * 1024 * 1024),
        cost_estimate=pl.CostEstimate(flops=0, bytes_accessed=size, transcendentals=0),
    )(*args)


def shape(dims, dtype=BF16):
    return jax.ShapeDtypeStruct(dims, dtype)


def shards(tokens, cotangent, routes, gate_probs, w_gate, w_up, w_down, tile_noise):
    nodes = lax.axis_size("node")
    local = lax.axis_size("local")
    chips = local // 2
    count, feats = tokens.shape
    slots = 2 * nodes
    gate, up, down, noise = w_gate[0], w_up[0], w_down[0], tile_noise[0]
    width, hid = gate.shape
    routes_t = routes.T
    same_core = [[2 * y + c for y in range(chips)] for c in range(2)]
    swap = [(i, i ^ 1) for i in range(local)]
    core = lax.rem(lax.axis_index("local"), 2).astype(jnp.int32).reshape(1)

    (sent,) = call(
        pack_kernel,
        [shape((8 * nodes, LANES))],
        routes_t, gate_probs.T, tokens.T, cotangent.T,
        limit=60,
    )
    got = lax.all_to_all(sent.reshape(nodes, 8, LANES), "node", 0, 0, tiled=True)
    half = width // 2
    later, _ = lax.optimization_barrier((core, sent))
    scaled = call(
        scale_kernel,
        [
            pltpu.HBM((3 * hid, half), BF16),
            pltpu.HBM((3 * hid, half), BF16),
            pltpu.HBM((half, 2 * hid), BF16),
            pltpu.HBM((half, 2 * hid), BF16),
            pltpu.HBM((width, hid), BF16),
        ],
        later, gate, up, down, noise,
        scalars=1,
        scratch=[pltpu.VMEM((width, 3 * hid), BF16), pltpu.VMEM((half, hid), BF16)],
    )
    got, scaled = lax.optimization_barrier((got, scaled))
    ahead_near, ahead_far, near, far, down_t = scaled
    xdy, prob = call(
        unpack_kernel,
        [shape((2 * feats, slots)), shape((8, slots), F32)],
        got.reshape(8 * nodes, LANES),
    )
    mine = lax.all_gather(xdy, "local", axis=0, axis_index_groups=same_core)
    other = lax.ppermute(mine, "local", swap)
    rows = feats + 16
    partial, ahead_far, near, far = call(
        first_kernel,
        [
            pltpu.VMEM((3 * hid, slots), F32),
            pltpu.VMEM((3 * hid, half), BF16),
            pltpu.VMEM((half, 2 * hid), BF16),
            pltpu.VMEM((half, 2 * hid), BF16),
        ],
        mine, ahead_near, ahead_far, near, far,
        scratch=[
            pltpu.VMEM((chips, 2 * feats, slots), BF16),
            pltpu.VMEM((3 * hid, half), BF16),
            pltpu.SemaphoreType.DMA((5,)),
        ],
        limit=56,
        held=pl.ANY,
    )
    keep, send, d_all = call(
        main_kernel,
        [shape((chips, rows, slots)), shape((chips, rows, slots)), shape((slots, 3 * hid))],
        partial, ahead_far, other, prob, near, far,
    )
    came = lax.ppermute(send, "local", swap)
    pair = (keep.astype(F32) + came.astype(F32)).astype(BF16)
    parts = lax.all_to_all(pair, "local", 0, 0, axis_index_groups=same_core, tiled=True)
    (noise_grad,) = call(
        noise_kernel,
        [shape(noise.shape, F32)],
        core, mine, other, d_all, gate, up, down_t,
        scalars=1,
        scratch=[pltpu.VMEM((width, slots), BF16), pltpu.VMEM((width, slots), BF16)],
    )
    (home,) = call(collect_kernel, [shape((4 * nodes, LANES))], parts)
    back = lax.all_to_all(home.reshape(nodes, 4, LANES), "node", 0, 0, tiled=True)
    token_t, probs_t = call(
        finish_kernel,
        [shape((feats, count)), shape((routes.shape[1], count))],
        back.reshape(4 * nodes, LANES),
        routes_t,
    )
    return token_t.T, probs_t.T, noise_grad[None]


def solution(mesh):
    in_specs = (
        P("node", "local"),
        P("node", "local"),
        P("node", None),
        P("node", None),
        P("node", None, "local"),
        P("node", None, "local"),
        P("node", "local", None),
        P("node", None, None, "local"),
    )
    out_specs = (P("node", "local"), P("node", None), P("node", None, None, "local"))
    return jax.shard_map(shards, mesh=mesh, in_specs=in_specs, out_specs=out_specs, check_vma=False)
```

```python
import math

import jax
import jax.numpy as jnp
from jax import lax
from jax.experimental import pallas as pl
from jax.experimental.pallas import tpu as pltpu
from jax.sharding import PartitionSpec as P

EXP_GROUP = 4
LANES = 128
TAIL = 16
FACTORS = 3
F32 = jnp.float32
F16 = jnp.float16
BF16 = jnp.bfloat16
ROWS_BY_ROWS = (((0,), (0,)), ((), ()))
LANES_BY_LANES = (((1,), (1,)), ((), ()))


def dot(a, b, dims=(((1,), (0,)), ((), ()))):
    return lax.dot_general(a, b, dims, preferred_element_type=F32)


def select_rows(routes_ref, per_group, copies, rows):
    top, tokens = routes_ref.shape
    row = lax.broadcasted_iota(jnp.int32, (rows, tokens), 0)
    first = lax.div(row, per_group) * EXP_GROUP
    slot = lax.rem(lax.div(row, copies), per_group // copies)
    matches = [routes_ref[j : j + 1, :] == first for j in range(top)]
    hit = jnp.zeros((rows, tokens), F32)
    for match in matches:
        hit = jnp.where(match, 1.0, hit)
    before = lax.broadcasted_iota(jnp.int32, (tokens, tokens), 0)
    after = lax.broadcasted_iota(jnp.int32, (tokens, tokens), 1)
    earlier = jnp.where(before < after, 1.0, 0.0).astype(BF16)
    rank = dot(hit.astype(BF16), earlier)
    chosen = jnp.where(rank == slot.astype(F32), hit, 0.0)
    return chosen, lax.rem(row, copies), matches


def pack_kernel(routes_ref, probs_ref, x_ref, dy_ref, out_ref):
    rows, lanes = out_ref.shape
    feats = x_ref.shape[0]
    chosen, block, matches = select_rows(routes_ref, 8, 4, rows)
    weight = jnp.zeros(chosen.shape, F32)
    for j, match in enumerate(matches):
        weight = jnp.where(match, probs_ref[j : j + 1, :].astype(F32), weight)
    weight = jnp.sum(weight * chosen, axis=1, keepdims=True)
    pad = jnp.zeros((4 * lanes - 2 * feats, lanes), BF16)
    both = jnp.concatenate([x_ref[...], dy_ref[...], pad], axis=0)
    picked = dot(chosen.astype(BF16), both, LANES_BY_LANES)
    out = jnp.zeros((rows, lanes), F32)
    for j in range(4):
        out = jnp.where(block == j, picked[:, j * lanes : (j + 1) * lanes], out)
    lane = lax.broadcasted_iota(jnp.int32, (rows, lanes), 1)
    out = jnp.where((block == 3) & (lane == 2 * feats - 3 * lanes), weight, out)
    out_ref[...] = out.astype(BF16)


def unpack_kernel(got_ref, xdy_ref, prob_ref):
    rows, lanes = got_ref.shape
    got = got_ref[...]
    row = lax.broadcasted_iota(jnp.int32, (rows, lanes), 0)
    col = lax.broadcasted_iota(jnp.int32, (rows, lanes), 1)
    parts = []
    for j in range(4):
        place = jnp.where(row == 4 * col + j, 1.0, 0.0).astype(BF16)
        parts.append(dot(got, place, ROWS_BY_ROWS))
    whole = jnp.concatenate(parts, axis=0)
    both = xdy_ref.shape[0] - TAIL
    feats = both // 2
    prob_ref[...] = whole[both : both + 8]
    undo = []
    for first in (0, feats):
        half = whole[first : first + feats]
        top = jnp.max(jnp.abs(half), axis=0, keepdims=True)
        raised = jnp.ones(top.shape, F32)
        for _ in range(FACTORS):
            factor = jnp.ones(top.shape, F32)
            for power in (256.0, 16.0, 4.0):
                fits = top * raised * power <= 32768.0
                raised = jnp.where(fits, raised * power, raised)
                factor = jnp.where(fits, factor / power, factor)
            undo.append(factor)
        xdy_ref[first : first + feats, :] = half * raised
    undo.append(jnp.ones((TAIL - 2 * FACTORS, lanes), F32))
    xdy_ref[both:, :] = jnp.concatenate(undo, axis=0)


def scale_kernel(
    after_ref, gate_ref, up_ref, down_ref, noise_ref, wide_ref, tall_ref, eff_down_ref, down_t_ref
):
    del after_ref
    blocks, lanes = noise_ref.shape[1:]
    for b in range(blocks):
        part = slice(b * lanes, (b + 1) * lanes)
        gate = gate_ref[part, :].astype(F32) * (1.0 + noise_ref[0, b : b + 1, :])
        up = up_ref[part, :].astype(F32) * (1.0 + noise_ref[1, b : b + 1, :])
        tall_ref[part, :lanes] = gate.astype(BF16)
        tall_ref[part, lanes:] = up.astype(BF16)
        wide_ref[:lanes, part] = gate.astype(BF16).T
        wide_ref[lanes:, part] = up.astype(BF16).T
        down = down_ref[:, part].T
        down_t_ref[part, :] = down
        back = down.astype(F32) * (1.0 + noise_ref[2, b : b + 1, :])
        eff_down_ref[:, part] = back.astype(BF16).T


def lower(rows_ref, x_ref, dy_ref):
    feats = (rows_ref.shape[1] - TAIL) // 2
    for i in range(rows_ref.shape[0]):
        for j, target in enumerate((x_ref, dy_ref)):
            first = 2 * feats + j * FACTORS
            undo = jnp.ones((1, rows_ref.shape[2]), F32)
            for k in range(FACTORS):
                undo = undo * rows_ref[i, first + k : first + k + 1, :].astype(F32)
            value = rows_ref[i, j * feats : (j + 1) * feats, :].astype(F32) * undo
            target[i * feats : (i + 1) * feats, :] = value.astype(BF16)


def main_kernel(
    core_ref, prob_ref, rows_hbm, wide_hbm, down_hbm, tall_hbm,
    keep_ref, send_ref, d_ref, rows_ref, wide_ref, down_ref, tall_ref, x_ref, dy_ref, sems,
):
    pairs = ((rows_hbm, rows_ref), (wide_hbm, wide_ref), (down_hbm, down_ref), (tall_hbm, tall_ref))
    moves = [
        pltpu.make_async_copy(source, target, sems.at[i])
        for i, (source, target) in enumerate(pairs)
    ]
    for move in moves:
        move.start()
    moves[0].wait()
    lower(rows_ref, x_ref, dy_ref)
    core = core_ref[0]
    hid = down_ref.shape[0]
    moves[1].wait()
    pre = dot(wide_ref[...], x_ref[...])
    moves[2].wait()
    back = dot(down_ref[...], dy_ref[...])
    pre_gate, pre_up = pre[:hid], pre[hid:]
    prob = prob_ref[0:1, :]
    sig = jax.nn.sigmoid(pre_gate)
    swish = pre_gate * sig
    hidden = (swish * pre_up).astype(BF16).astype(F32)
    grad_hidden = prob * back
    d_gate = grad_hidden * pre_up * sig * (1.0 + pre_gate * (1.0 - sig))
    d_up = grad_hidden * swish
    d_ref[:, :hid] = d_gate.T.astype(BF16)
    d_ref[:, hid : 2 * hid] = d_up.T.astype(BF16)
    d_ref[:, 2 * hid :] = (prob * hidden).T.astype(BF16)
    d_both = jnp.concatenate([d_gate.astype(BF16), d_up.astype(BF16)], axis=0)
    prob_term = jnp.sum(hidden * back, axis=0, keepdims=True)
    chips, rows, lanes = keep_ref.shape
    feats = x_ref.shape[0] // (2 * chips)
    line = lax.broadcasted_iota(jnp.int32, (rows - feats, lanes), 0)
    tail = jnp.where(line == 0, prob_term, 0.0).astype(BF16)
    moves[3].wait()
    for chip in range(chips):
        for target, rank in ((send_ref, 1 - core), (keep_ref, core)):
            start = pl.multiple_of((2 * chip + rank) * feats, 32)
            target[chip, :feats, :] = dot(tall_ref[pl.ds(start, feats), :], d_both).astype(BF16)
            target[chip, feats:, :] = tail


def noise_kernel(rows_ref, d_ref, gate_ref, up_ref, down_t_ref, out_ref, x_ref, dy_ref):
    lower(rows_ref, x_ref, dy_ref)
    blocks, lanes = out_ref.shape[1:]
    for b in range(blocks):
        part = slice(b * lanes, (b + 1) * lanes)
        grad = dot(x_ref[part, :], d_ref[:, : 2 * lanes])
        grad_down = dot(dy_ref[part, :], d_ref[:, 2 * lanes :])
        pieces = (
            (gate_ref, grad[:, :lanes]),
            (up_ref, grad[:, lanes:]),
            (down_t_ref, grad_down),
        )
        for i, (weight, value) in enumerate(pieces):
            out_ref[i, b : b + 1, :] = jnp.sum(
                weight[part, :].astype(F32) * value, axis=0, keepdims=True
            )


def collect_kernel(parts_ref, out_ref):
    rows, lanes = out_ref.shape
    chips, height, slots = parts_ref.shape
    total = parts_ref[0].astype(F32)
    for chip in range(1, chips):
        total = total + parts_ref[chip].astype(F32)
    pad = jnp.zeros((2 * lanes - height, slots), BF16)
    total = jnp.concatenate([total.astype(BF16), pad], axis=0)
    row = lax.broadcasted_iota(jnp.int32, (rows, slots), 0)
    col = lax.broadcasted_iota(jnp.int32, (rows, slots), 1)
    place = jnp.where(lax.div(row, 2) == col, 1.0, 0.0).astype(BF16)
    spread = dot(place, total, LANES_BY_LANES)
    odd = lax.rem(lax.broadcasted_iota(jnp.int32, (rows, lanes), 0), 2)
    out_ref[...] = jnp.where(odd == 0, spread[:, :lanes], spread[:, lanes:]).astype(BF16)


def finish_kernel(back_ref, routes_ref, tokens_ref, probs_ref):
    rows, lanes = back_ref.shape
    feats = tokens_ref.shape[0]
    chosen, block, matches = select_rows(routes_ref, 4, 2, rows)
    back = back_ref[...]
    low = dot(back, jnp.where(block == 0, chosen, 0.0).astype(BF16), ROWS_BY_ROWS)
    high_rows = jnp.where(block == 1, chosen, 0.0)
    high = dot(back, high_rows.astype(BF16), ROWS_BY_ROWS)
    tokens_ref[:lanes, :] = low.astype(BF16)
    tokens_ref[lanes:, :] = high[: feats - lanes].astype(BF16)
    given = back[:, feats - lanes : feats - lanes + 1].astype(F32) * high_rows
    lines = [
        jnp.sum(jnp.where(match, given, 0.0), axis=0, keepdims=True) for match in matches
    ]
    probs_ref[...] = jnp.concatenate(lines, axis=0).astype(BF16)


def call(kernel, outs, *args, scalars=0, scratch=(), limit=32, far=0):
    size = sum(math.prod(a.shape) * a.dtype.itemsize for a in [*args, *outs])
    specs = [pl.BlockSpec(memory_space=pltpu.SMEM)] * scalars
    specs += [pl.BlockSpec(memory_space=pltpu.VMEM)] * (len(args) - scalars - far)
    specs += [pl.BlockSpec(memory_space=pl.ANY)] * far
    return pl.pallas_call(
        kernel,
        out_shape=outs,
        in_specs=specs,
        out_specs=[pl.BlockSpec(memory_space=pltpu.VMEM)] * len(outs),
        scratch_shapes=list(scratch),
        compiler_params=pltpu.CompilerParams(vmem_limit_bytes=limit * 1024 * 1024),
        cost_estimate=pl.CostEstimate(flops=0, bytes_accessed=size, transcendentals=0),
    )(*args)


def shape(dims, dtype=BF16):
    return jax.ShapeDtypeStruct(dims, dtype)


def shards(tokens, cotangent, routes, gate_probs, w_gate, w_up, w_down, tile_noise):
    nodes = lax.axis_size("node")
    local = lax.axis_size("local")
    chips = local // 2
    count, feats = tokens.shape
    slots = 2 * nodes
    gate, up, down, noise = w_gate[0], w_up[0], w_down[0], tile_noise[0]
    width, hid = gate.shape
    routes_t = routes.T
    same_core = [[2 * y + c for y in range(chips)] for c in range(2)]
    swap = [(i, i ^ 1) for i in range(local)]
    core = lax.rem(lax.axis_index("local"), 2).astype(jnp.int32).reshape(1)

    (sent,) = call(
        pack_kernel,
        [shape((8 * nodes, LANES))],
        routes_t, gate_probs.T, tokens.T, cotangent.T,
        limit=60,
    )
    got = lax.all_to_all(sent.reshape(nodes, 8, LANES), "node", 0, 0, tiled=True)
    later, _ = lax.optimization_barrier((core, sent))
    scaled = call(
        scale_kernel,
        [
            pltpu.HBM((2 * hid, width), BF16),
            pltpu.HBM((width, 2 * hid), BF16),
            pltpu.HBM((hid, width), BF16),
            pltpu.HBM((width, hid), BF16),
        ],
        later, gate, up, down, noise,
        scalars=1,
    )
    got, scaled = lax.optimization_barrier((got, scaled))
    wide, tall, eff_down, down_t = scaled
    xdy, prob = call(
        unpack_kernel,
        [shape((2 * feats + TAIL, slots), F32), shape((8, slots), F32)],
        got.reshape(8 * nodes, LANES),
    )
    rows = lax.all_gather(xdy.astype(F16), "local", axis=0).astype(BF16)
    high = feats + 16
    keep, send, d_all = call(
        main_kernel,
        [
            pltpu.VMEM((chips, high, slots), BF16),
            pltpu.VMEM((chips, high, slots), BF16),
            pltpu.VMEM((slots, 3 * hid), BF16),
        ],
        core, prob, rows, wide, eff_down, tall,
        scalars=1,
        scratch=[
            pltpu.VMEM(rows.shape, BF16),
            pltpu.VMEM((2 * hid, width), BF16),
            pltpu.VMEM((hid, width), BF16),
            pltpu.VMEM((width, 2 * hid), BF16),
            pltpu.VMEM((width, slots), BF16),
            pltpu.VMEM((width, slots), BF16),
            pltpu.SemaphoreType.DMA((4,)),
        ],
        far=4,
        limit=57,
    )
    came = lax.ppermute(send, "local", swap)
    pair = (keep.astype(F32) + came.astype(F32)).astype(BF16)
    parts = lax.all_to_all(pair, "local", 0, 0, axis_index_groups=same_core, tiled=True)
    (noise_grad,) = call(
        noise_kernel,
        [shape(noise.shape, F32)],
        rows, d_all, gate, up, down_t,
        scratch=[pltpu.VMEM((width, slots), BF16), pltpu.VMEM((width, slots), BF16)],
    )
    (home,) = call(collect_kernel, [shape((4 * nodes, LANES))], parts)
    back = lax.all_to_all(home.reshape(nodes, 4, LANES), "node", 0, 0, tiled=True)
    token_t, probs_t = call(
        finish_kernel,
        [shape((feats, count)), shape((routes.shape[1], count))],
        back.reshape(4 * nodes, LANES),
        routes_t,
    )
    return token_t.T, probs_t.T, noise_grad[None]


def solution(mesh):
    in_specs = (
        P("node", "local"),
        P("node", "local"),
        P("node", None),
        P("node", None),
        P("node", None, "local"),
        P("node", None, "local"),
        P("node", "local", None),
        P("node", None, None, "local"),
    )
    out_specs = (P("node", "local"), P("node", None), P("node", None, None, "local"))
    return jax.shard_map(shards, mesh=mesh, in_specs=in_specs, out_specs=out_specs, check_vma=False)
```

```python
import math

import jax
import jax.numpy as jnp
from jax import lax
from jax.experimental import pallas as pl
from jax.experimental.pallas import tpu as pltpu
from jax.sharding import PartitionSpec as P

EXP_GROUP = 4
LANES = 128
TAIL = 16
FACTORS = 3
held = pltpu.with_memory_space_constraint
F32 = jnp.float32
F16 = jnp.float16
BF16 = jnp.bfloat16
ROWS_BY_ROWS = (((0,), (0,)), ((), ()))
LANES_BY_LANES = (((1,), (1,)), ((), ()))


def dot(a, b, dims=(((1,), (0,)), ((), ()))):
    return lax.dot_general(a, b, dims, preferred_element_type=F32)


def select_rows(routes_ref, per_group, copies, rows):
    top, tokens = routes_ref.shape
    row = lax.broadcasted_iota(jnp.int32, (rows, tokens), 0)
    first = lax.div(row, per_group) * EXP_GROUP
    slot = lax.rem(lax.div(row, copies), per_group // copies)
    matches = [routes_ref[j : j + 1, :] == first for j in range(top)]
    hit = jnp.zeros((rows, tokens), F32)
    for match in matches:
        hit = jnp.where(match, 1.0, hit)
    before = lax.broadcasted_iota(jnp.int32, (tokens, tokens), 0)
    after = lax.broadcasted_iota(jnp.int32, (tokens, tokens), 1)
    earlier = jnp.where(before < after, 1.0, 0.0).astype(BF16)
    rank = dot(hit.astype(BF16), earlier)
    chosen = jnp.where(rank == slot.astype(F32), hit, 0.0)
    return chosen, lax.rem(row, copies), matches


def pack_kernel(
    routes_hbm, probs_hbm, x_hbm, dy_hbm, out_ref, routes_ref, probs_ref, x_ref, dy_ref, sems
):
    pairs = (
        (routes_hbm, routes_ref),
        (probs_hbm, probs_ref),
        (x_hbm, x_ref),
        (dy_hbm, dy_ref),
    )
    moves = [
        pltpu.make_async_copy(source, target, sems.at[i])
        for i, (source, target) in enumerate(pairs)
    ]
    for move in moves:
        move.start()
    rows, lanes = out_ref.shape
    for move in moves[:2]:
        move.wait()
    feats = x_ref.shape[0]
    chosen, block, matches = select_rows(routes_ref, 8, 4, rows)
    weight = jnp.zeros(chosen.shape, F32)
    for j, match in enumerate(matches):
        weight = jnp.where(match, probs_ref[j : j + 1, :].astype(F32), weight)
    weight = jnp.sum(weight * chosen, axis=1, keepdims=True)
    for move in moves[2:]:
        move.wait()
    pad = jnp.zeros((4 * lanes - 2 * feats, lanes), BF16)
    both = jnp.concatenate([x_ref[...], dy_ref[...], pad], axis=0)
    picked = dot(chosen.astype(BF16), both, LANES_BY_LANES)
    out = jnp.zeros((rows, lanes), F32)
    for j in range(4):
        out = jnp.where(block == j, picked[:, j * lanes : (j + 1) * lanes], out)
    lane = lax.broadcasted_iota(jnp.int32, (rows, lanes), 1)
    out = jnp.where((block == 3) & (lane == 2 * feats - 3 * lanes), weight, out)
    out_ref[...] = out.astype(BF16)


def unpack_kernel(got_ref, xdy_ref, prob_ref):
    rows, lanes = got_ref.shape
    got = got_ref[...]
    row = lax.broadcasted_iota(jnp.int32, (rows, lanes), 0)
    col = lax.broadcasted_iota(jnp.int32, (rows, lanes), 1)
    parts = []
    for j in range(4):
        place = jnp.where(row == 4 * col + j, 1.0, 0.0).astype(BF16)
        parts.append(dot(got, place, ROWS_BY_ROWS))
    whole = jnp.concatenate(parts, axis=0)
    both = xdy_ref.shape[0] - TAIL
    feats = both // 2
    prob_ref[...] = whole[both : both + 8]
    undo = []
    for first in (0, feats):
        half = whole[first : first + feats]
        top = jnp.max(jnp.abs(half), axis=0, keepdims=True)
        raised = jnp.ones(top.shape, F32)
        for _ in range(FACTORS):
            factor = jnp.ones(top.shape, F32)
            for power in (256.0, 16.0, 4.0):
                fits = top * raised * power <= 32768.0
                raised = jnp.where(fits, raised * power, raised)
                factor = jnp.where(fits, factor / power, factor)
            undo.append(factor)
        xdy_ref[first : first + feats, :] = half * raised
    undo.append(jnp.ones((TAIL - 2 * FACTORS, lanes), F32))
    xdy_ref[both:, :] = jnp.concatenate(undo, axis=0)


def scale_kernel(
    after_ref, gate_ref, up_ref, down_ref, noise_ref, wide_ref, tall_ref, eff_down_ref, down_t_ref
):
    del after_ref
    blocks, lanes = noise_ref.shape[1:]
    for b in range(blocks):
        part = slice(b * lanes, (b + 1) * lanes)
        gate = gate_ref[part, :].astype(F32) * (1.0 + noise_ref[0, b : b + 1, :])
        up = up_ref[part, :].astype(F32) * (1.0 + noise_ref[1, b : b + 1, :])
        tall_ref[part, :lanes] = gate.astype(BF16)
        tall_ref[part, lanes:] = up.astype(BF16)
        wide_ref[:lanes, part] = gate.astype(BF16).T
        wide_ref[lanes:, part] = up.astype(BF16).T
        down = down_ref[:, part].T
        down_t_ref[part, :] = down
        back = down.astype(F32) * (1.0 + noise_ref[2, b : b + 1, :])
        eff_down_ref[:, part] = back.astype(BF16).T


def lower(rows_ref, x_ref, dy_ref):
    feats = (rows_ref.shape[1] - TAIL) // 2
    for i in range(rows_ref.shape[0]):
        for j, target in enumerate((x_ref, dy_ref)):
            first = 2 * feats + j * FACTORS
            undo = jnp.ones((1, rows_ref.shape[2]), F32)
            for k in range(FACTORS):
                undo = undo * rows_ref[i, first + k : first + k + 1, :].astype(F32)
            value = rows_ref[i, j * feats : (j + 1) * feats, :].astype(F32) * undo
            target[i * feats : (i + 1) * feats, :] = value.astype(BF16)


def main_kernel(
    core_ref, prob_ref, rows_ref, wide_hbm, down_hbm, tall_hbm,
    keep_ref, send_ref, d_ref, wide_ref, down_ref, tall_ref, x_ref, dy_ref, sems,
):
    pairs = ((wide_hbm, wide_ref), (down_hbm, down_ref), (tall_hbm, tall_ref))
    moves = [
        pltpu.make_async_copy(source, target, sems.at[i])
        for i, (source, target) in enumerate(pairs)
    ]
    for move in moves:
        move.start()
    lower(rows_ref, x_ref, dy_ref)
    core = core_ref[0]
    hid = down_ref.shape[0]
    moves[0].wait()
    pre = dot(wide_ref[...], x_ref[...])
    moves[1].wait()
    back = dot(down_ref[...], dy_ref[...])
    pre_gate, pre_up = pre[:hid], pre[hid:]
    prob = prob_ref[0:1, :]
    sig = jax.nn.sigmoid(pre_gate)
    swish = pre_gate * sig
    hidden = (swish * pre_up).astype(BF16).astype(F32)
    grad_hidden = prob * back
    d_gate = grad_hidden * pre_up * sig * (1.0 + pre_gate * (1.0 - sig))
    d_up = grad_hidden * swish
    d_ref[:, :hid] = d_gate.T.astype(BF16)
    d_ref[:, hid : 2 * hid] = d_up.T.astype(BF16)
    d_ref[:, 2 * hid :] = (prob * hidden).T.astype(BF16)
    d_both = jnp.concatenate([d_gate.astype(BF16), d_up.astype(BF16)], axis=0)
    prob_term = jnp.sum(hidden * back, axis=0, keepdims=True)
    chips, rows, lanes = keep_ref.shape
    feats = x_ref.shape[0] // (2 * chips)
    line = lax.broadcasted_iota(jnp.int32, (rows - feats, lanes), 0)
    tail = jnp.where(line == 0, prob_term, 0.0).astype(BF16)
    moves[2].wait()
    for chip in range(chips):
        for target, rank in ((send_ref, 1 - core), (keep_ref, core)):
            start = pl.multiple_of((2 * chip + rank) * feats, 32)
            target[chip, :feats, :] = dot(tall_ref[pl.ds(start, feats), :], d_both).astype(BF16)
            target[chip, feats:, :] = tail


def noise_kernel(rows_ref, d_ref, gate_ref, up_ref, down_t_ref, out_ref, x_ref, dy_ref):
    lower(rows_ref, x_ref, dy_ref)
    blocks, lanes = out_ref.shape[1:]
    for b in range(blocks):
        part = slice(b * lanes, (b + 1) * lanes)
        grad = dot(x_ref[part, :], d_ref[:, : 2 * lanes])
        grad_down = dot(dy_ref[part, :], d_ref[:, 2 * lanes :])
        pieces = (
            (gate_ref, grad[:, :lanes]),
            (up_ref, grad[:, lanes:]),
            (down_t_ref, grad_down),
        )
        for i, (weight, value) in enumerate(pieces):
            out_ref[i, b : b + 1, :] = jnp.sum(
                weight[part, :].astype(F32) * value, axis=0, keepdims=True
            )


def collect_kernel(parts_ref, out_ref):
    rows, lanes = out_ref.shape
    chips, height, slots = parts_ref.shape
    total = parts_ref[0].astype(F32)
    for chip in range(1, chips):
        total = total + parts_ref[chip].astype(F32)
    pad = jnp.zeros((2 * lanes - height, slots), BF16)
    total = jnp.concatenate([total.astype(BF16), pad], axis=0)
    row = lax.broadcasted_iota(jnp.int32, (rows, slots), 0)
    col = lax.broadcasted_iota(jnp.int32, (rows, slots), 1)
    place = jnp.where(lax.div(row, 2) == col, 1.0, 0.0).astype(BF16)
    spread = dot(place, total, LANES_BY_LANES)
    odd = lax.rem(lax.broadcasted_iota(jnp.int32, (rows, lanes), 0), 2)
    out_ref[...] = jnp.where(odd == 0, spread[:, :lanes], spread[:, lanes:]).astype(BF16)


def choose_kernel(routes_ref, out_ref):
    rows = out_ref.shape[0]
    tokens = routes_ref.shape[1]
    chosen, block, matches = select_rows(routes_ref, 4, 2, rows)
    high = jnp.where(block == 1, chosen, 0.0)
    masks = [jnp.where(block == 0, chosen, 0.0), high]
    masks += [jnp.where(match, high, 0.0) for match in matches]
    for i, mask in enumerate(masks):
        out_ref[:, i * tokens : (i + 1) * tokens] = mask.astype(BF16)


def finish_kernel(back_ref, chosen_ref, tokens_ref, probs_ref):
    lanes = back_ref.shape[1]
    feats, tokens = tokens_ref.shape
    out = dot(back_ref[...], chosen_ref[...], ROWS_BY_ROWS)
    tokens_ref[:lanes, :] = out[:, :tokens].astype(BF16)
    tokens_ref[lanes:, :] = out[: feats - lanes, tokens : 2 * tokens].astype(BF16)
    line = feats - lanes
    for j in range(probs_ref.shape[0]):
        part = slice((2 + j) * tokens, (3 + j) * tokens)
        probs_ref[j : j + 1, :] = out[line : line + 1, part].astype(BF16)


def call(kernel, outs, *args, scalars=0, scratch=(), limit=32, far=0):
    size = sum(math.prod(a.shape) * a.dtype.itemsize for a in [*args, *outs])
    specs = [pl.BlockSpec(memory_space=pltpu.SMEM)] * scalars
    specs += [pl.BlockSpec(memory_space=pltpu.VMEM)] * (len(args) - scalars - far)
    specs += [pl.BlockSpec(memory_space=pl.ANY)] * far
    return pl.pallas_call(
        kernel,
        out_shape=outs,
        in_specs=specs,
        out_specs=[pl.BlockSpec(memory_space=pltpu.VMEM)] * len(outs),
        scratch_shapes=list(scratch),
        compiler_params=pltpu.CompilerParams(vmem_limit_bytes=limit * 1024 * 1024),
        cost_estimate=pl.CostEstimate(flops=0, bytes_accessed=size, transcendentals=0),
    )(*args)


def shape(dims, dtype=BF16):
    return jax.ShapeDtypeStruct(dims, dtype)


def shards(tokens, cotangent, routes, gate_probs, w_gate, w_up, w_down, tile_noise):
    nodes = lax.axis_size("node")
    local = lax.axis_size("local")
    chips = local // 2
    count, feats = tokens.shape
    slots = 2 * nodes
    gate, up, down, noise = w_gate[0], w_up[0], w_down[0], tile_noise[0]
    width, hid = gate.shape
    routes_t = routes.T
    same_core = [[2 * y + c for y in range(chips)] for c in range(2)]
    swap = [(i, i ^ 1) for i in range(local)]
    core = lax.rem(lax.axis_index("local"), 2).astype(jnp.int32).reshape(1)

    given = (routes_t, gate_probs.T, tokens.T, cotangent.T)
    (sent,) = call(
        pack_kernel,
        [pltpu.VMEM((8 * nodes, LANES), BF16)],
        *[held(a, pltpu.HBM) for a in given],
        scratch=[pltpu.VMEM(a.shape, a.dtype) for a in given] + [pltpu.SemaphoreType.DMA((4,))],
        far=4,
    )
    got = lax.all_to_all(sent.reshape(nodes, 8, LANES), "node", 0, 0, tiled=True)
    later, _ = lax.optimization_barrier((core, sent))
    scaled = call(
        scale_kernel,
        [
            pltpu.HBM((2 * hid, width), BF16),
            pltpu.HBM((width, 2 * hid), BF16),
            pltpu.HBM((hid, width), BF16),
            pltpu.HBM((width, hid), BF16),
        ],
        later, gate, up, down, noise,
        scalars=1,
    )
    got, scaled = lax.optimization_barrier((got, scaled))
    wide, tall, eff_down, down_t = scaled
    xdy, prob = call(
        unpack_kernel,
        [shape((2 * feats + TAIL, slots), F32), shape((8, slots), F32)],
        got.reshape(8 * nodes, LANES),
    )
    rows = lax.all_gather(xdy.astype(F16), "local", axis=0).astype(BF16)
    high = feats + 16
    keep, send, d_all = call(
        main_kernel,
        [
            pltpu.VMEM((chips, high, slots), BF16),
            pltpu.VMEM((chips, high, slots), BF16),
            pltpu.VMEM((slots, 3 * hid), BF16),
        ],
        core, prob, held(rows, pltpu.VMEM), *[held(a, pltpu.HBM) for a in (wide, eff_down, tall)],
        scalars=1,
        scratch=[
            pltpu.VMEM((2 * hid, width), BF16),
            pltpu.VMEM((hid, width), BF16),
            pltpu.VMEM((width, 2 * hid), BF16),
            pltpu.VMEM((width, slots), BF16),
            pltpu.VMEM((width, slots), BF16),
            pltpu.SemaphoreType.DMA((3,)),
        ],
        far=3,
    )
    came = lax.ppermute(send, "local", swap)
    pair = (keep.astype(F32) + came.astype(F32)).astype(BF16)
    parts = lax.all_to_all(pair, "local", 0, 0, axis_index_groups=same_core, tiled=True)
    (noise_grad,) = call(
        noise_kernel,
        [shape(noise.shape, F32)],
        rows, d_all, gate, up, down_t,
        scratch=[pltpu.VMEM((width, slots), BF16), pltpu.VMEM((width, slots), BF16)],
    )
    (home,) = call(collect_kernel, [shape((4 * nodes, LANES))], parts)
    routes_later, home = lax.optimization_barrier((routes_t, home))
    back = lax.all_to_all(home.reshape(nodes, 4, LANES), "node", 0, 0, tiled=True)
    top = routes.shape[1]
    (chosen,) = call(choose_kernel, [shape((4 * nodes, (2 + top) * count))], routes_later)
    token_t, probs_t = call(
        finish_kernel,
        [shape((feats, count)), shape((top, count))],
        back.reshape(4 * nodes, LANES),
        chosen,
    )
    return token_t.T, probs_t.T, noise_grad[None]


def solution(mesh):
    in_specs = (
        P("node", "local"),
        P("node", "local"),
        P("node", None),
        P("node", None),
        P("node", None, "local"),
        P("node", None, "local"),
        P("node", "local", None),
        P("node", None, None, "local"),
    )
    out_specs = (P("node", "local"), P("node", None), P("node", None, None, "local"))
    return jax.shard_map(shards, mesh=mesh, in_specs=in_specs, out_specs=out_specs, check_vma=False)
```

```python
import math

import jax
import jax.numpy as jnp
from jax import lax
from jax.experimental import pallas as pl
from jax.experimental.pallas import tpu as pltpu
from jax.sharding import PartitionSpec as P

EXP_GROUP = 4
LANES = 128
TAIL = 16
FACTORS = 3
held = pltpu.with_memory_space_constraint
F32 = jnp.float32
F16 = jnp.float16
BF16 = jnp.bfloat16
ROWS_BY_ROWS = (((0,), (0,)), ((), ()))
LANES_BY_LANES = (((1,), (1,)), ((), ()))


def dot(a, b, dims=(((1,), (0,)), ((), ()))):
    return lax.dot_general(a, b, dims, preferred_element_type=F32)


def select_rows(routes_ref, per_group, copies, rows):
    top, tokens = routes_ref.shape
    row = lax.broadcasted_iota(jnp.int32, (rows, tokens), 0)
    first = lax.div(row, per_group) * EXP_GROUP
    slot = lax.rem(lax.div(row, copies), per_group // copies)
    matches = [routes_ref[j : j + 1, :] == first for j in range(top)]
    hit = jnp.zeros((rows, tokens), F32)
    for match in matches:
        hit = jnp.where(match, 1.0, hit)
    before = lax.broadcasted_iota(jnp.int32, (tokens, tokens), 0)
    after = lax.broadcasted_iota(jnp.int32, (tokens, tokens), 1)
    earlier = jnp.where(before < after, 1.0, 0.0).astype(BF16)
    rank = dot(hit.astype(BF16), earlier)
    chosen = jnp.where(rank == slot.astype(F32), hit, 0.0)
    return chosen, lax.rem(row, copies), matches


def pack_kernel(
    routes_hbm, probs_hbm, x_hbm, dy_hbm, out_ref, routes_ref, probs_ref, x_ref, dy_ref, sems
):
    pairs = (
        (routes_hbm, routes_ref),
        (probs_hbm, probs_ref),
        (x_hbm, x_ref),
        (dy_hbm, dy_ref),
    )
    moves = [
        pltpu.make_async_copy(source, target, sems.at[i])
        for i, (source, target) in enumerate(pairs)
    ]
    for move in moves:
        move.start()
    rows, lanes = out_ref.shape
    for move in moves[:2]:
        move.wait()
    feats = x_ref.shape[0]
    chosen, block, matches = select_rows(routes_ref, 8, 4, rows)
    weight = jnp.zeros(chosen.shape, F32)
    for j, match in enumerate(matches):
        weight = jnp.where(match, probs_ref[j : j + 1, :].astype(F32), weight)
    weight = jnp.sum(weight * chosen, axis=1, keepdims=True)
    for move in moves[2:]:
        move.wait()
    pad = jnp.zeros((4 * lanes - 2 * feats, lanes), BF16)
    both = jnp.concatenate([x_ref[...], dy_ref[...], pad], axis=0)
    picked = dot(chosen.astype(BF16), both, LANES_BY_LANES)
    out = jnp.zeros((rows, lanes), F32)
    for j in range(4):
        out = jnp.where(block == j, picked[:, j * lanes : (j + 1) * lanes], out)
    lane = lax.broadcasted_iota(jnp.int32, (rows, lanes), 1)
    out = jnp.where((block == 3) & (lane == 2 * feats - 3 * lanes), weight, out)
    out_ref[...] = out.astype(BF16)


def unpack_kernel(got_ref, xdy_ref, prob_ref):
    rows, lanes = got_ref.shape
    got = got_ref[...]
    row = lax.broadcasted_iota(jnp.int32, (rows, lanes), 0)
    col = lax.broadcasted_iota(jnp.int32, (rows, lanes), 1)
    parts = []
    for j in range(4):
        place = jnp.where(row == 4 * col + j, 1.0, 0.0).astype(BF16)
        parts.append(dot(got, place, ROWS_BY_ROWS))
    whole = jnp.concatenate(parts, axis=0)
    both = xdy_ref.shape[0] - TAIL
    feats = both // 2
    prob_ref[...] = whole[both : both + 8]
    undo = []
    for first in (0, feats):
        half = whole[first : first + feats]
        top = jnp.max(jnp.abs(half), axis=0, keepdims=True)
        raised = jnp.ones(top.shape, F32)
        for _ in range(FACTORS):
            factor = jnp.ones(top.shape, F32)
            for power in (256.0, 16.0, 4.0):
                fits = top * raised * power <= 32768.0
                raised = jnp.where(fits, raised * power, raised)
                factor = jnp.where(fits, factor / power, factor)
            undo.append(factor)
        xdy_ref[first : first + feats, :] = half * raised
    undo.append(jnp.ones((TAIL - 2 * FACTORS, lanes), F32))
    xdy_ref[both:, :] = jnp.concatenate(undo, axis=0)


def scale_kernel(
    after_ref, gate_ref, up_ref, down_ref, noise_ref, tall_ref, eff_down_ref, down_t_ref
):
    del after_ref
    blocks, lanes = noise_ref.shape[1:]
    for b in range(blocks):
        part = slice(b * lanes, (b + 1) * lanes)
        gate = gate_ref[part, :].astype(F32) * (1.0 + noise_ref[0, b : b + 1, :])
        up = up_ref[part, :].astype(F32) * (1.0 + noise_ref[1, b : b + 1, :])
        tall_ref[part, :lanes] = gate.astype(BF16)
        tall_ref[part, lanes:] = up.astype(BF16)
        down = down_ref[:, part].T
        down_t_ref[part, :] = down
        back = down.astype(F32) * (1.0 + noise_ref[2, b : b + 1, :])
        eff_down_ref[:, part] = back.astype(BF16).T


def lower(rows_ref, x_ref, dy_ref):
    feats = (rows_ref.shape[1] - TAIL) // 2
    for i in range(rows_ref.shape[0]):
        for j, target in enumerate((x_ref, dy_ref)):
            first = 2 * feats + j * FACTORS
            undo = jnp.ones((1, rows_ref.shape[2]), F32)
            for k in range(FACTORS):
                undo = undo * rows_ref[i, first + k : first + k + 1, :].astype(F32)
            value = rows_ref[i, j * feats : (j + 1) * feats, :].astype(F32) * undo
            target[i * feats : (i + 1) * feats, :] = value.astype(BF16)


def main_kernel(
    core_ref, prob_ref, rows_ref, tall_hbm, down_hbm,
    keep_ref, send_ref, d_ref, tall_ref, down_ref, x_ref, dy_ref, sems,
):
    pairs = ((tall_hbm, tall_ref), (down_hbm, down_ref))
    moves = [
        pltpu.make_async_copy(source, target, sems.at[i])
        for i, (source, target) in enumerate(pairs)
    ]
    for move in moves:
        move.start()
    lower(rows_ref, x_ref, dy_ref)
    core = core_ref[0]
    hid = down_ref.shape[0]
    moves[0].wait()
    pre = dot(x_ref[...], tall_ref[...], ROWS_BY_ROWS).T
    moves[1].wait()
    back = dot(down_ref[...], dy_ref[...])
    pre_gate, pre_up = pre[:hid], pre[hid:]
    prob = prob_ref[0:1, :]
    sig = jax.nn.sigmoid(pre_gate)
    swish = pre_gate * sig
    hidden = (swish * pre_up).astype(BF16).astype(F32)
    grad_hidden = prob * back
    d_gate = grad_hidden * pre_up * sig * (1.0 + pre_gate * (1.0 - sig))
    d_up = grad_hidden * swish
    d_ref[:, :hid] = d_gate.T.astype(BF16)
    d_ref[:, hid : 2 * hid] = d_up.T.astype(BF16)
    d_ref[:, 2 * hid :] = (prob * hidden).T.astype(BF16)
    d_both = jnp.concatenate([d_gate.astype(BF16), d_up.astype(BF16)], axis=0)
    prob_term = jnp.sum(hidden * back, axis=0, keepdims=True)
    chips, rows, lanes = keep_ref.shape
    feats = x_ref.shape[0] // (2 * chips)
    line = lax.broadcasted_iota(jnp.int32, (rows - feats, lanes), 0)
    tail = jnp.where(line == 0, prob_term, 0.0).astype(BF16)
    for chip in range(chips):
        for target, rank in ((send_ref, 1 - core), (keep_ref, core)):
            start = pl.multiple_of((2 * chip + rank) * feats, 32)
            target[chip, :feats, :] = dot(tall_ref[pl.ds(start, feats), :], d_both).astype(BF16)
            target[chip, feats:, :] = tail


def noise_kernel(rows_ref, d_ref, gate_ref, up_ref, down_t_ref, out_ref, x_ref, dy_ref):
    lower(rows_ref, x_ref, dy_ref)
    blocks, lanes = out_ref.shape[1:]
    for b in range(blocks):
        part = slice(b * lanes, (b + 1) * lanes)
        grad = dot(x_ref[part, :], d_ref[:, : 2 * lanes])
        grad_down = dot(dy_ref[part, :], d_ref[:, 2 * lanes :])
        pieces = (
            (gate_ref, grad[:, :lanes]),
            (up_ref, grad[:, lanes:]),
            (down_t_ref, grad_down),
        )
        for i, (weight, value) in enumerate(pieces):
            out_ref[i, b : b + 1, :] = jnp.sum(
                weight[part, :].astype(F32) * value, axis=0, keepdims=True
            )


def collect_kernel(parts_ref, out_ref):
    rows, lanes = out_ref.shape
    chips, height, slots = parts_ref.shape
    total = parts_ref[0].astype(F32)
    for chip in range(1, chips):
        total = total + parts_ref[chip].astype(F32)
    pad = jnp.zeros((2 * lanes - height, slots), BF16)
    total = jnp.concatenate([total.astype(BF16), pad], axis=0)
    row = lax.broadcasted_iota(jnp.int32, (rows, slots), 0)
    col = lax.broadcasted_iota(jnp.int32, (rows, slots), 1)
    place = jnp.where(lax.div(row, 2) == col, 1.0, 0.0).astype(BF16)
    spread = dot(place, total, LANES_BY_LANES)
    odd = lax.rem(lax.broadcasted_iota(jnp.int32, (rows, lanes), 0), 2)
    out_ref[...] = jnp.where(odd == 0, spread[:, :lanes], spread[:, lanes:]).astype(BF16)


def choose_kernel(routes_ref, out_ref):
    rows = out_ref.shape[0]
    tokens = routes_ref.shape[1]
    chosen, block, matches = select_rows(routes_ref, 4, 2, rows)
    high = jnp.where(block == 1, chosen, 0.0)
    masks = [jnp.where(block == 0, chosen, 0.0), high]
    masks += [jnp.where(match, high, 0.0) for match in matches]
    for i, mask in enumerate(masks):
        out_ref[:, i * tokens : (i + 1) * tokens] = mask.astype(BF16)


def finish_kernel(back_ref, chosen_ref, tokens_ref, probs_ref):
    lanes = back_ref.shape[1]
    feats, tokens = tokens_ref.shape
    out = dot(back_ref[...], chosen_ref[...], ROWS_BY_ROWS)
    tokens_ref[:lanes, :] = out[:, :tokens].astype(BF16)
    tokens_ref[lanes:, :] = out[: feats - lanes, tokens : 2 * tokens].astype(BF16)
    line = feats - lanes
    for j in range(probs_ref.shape[0]):
        part = slice((2 + j) * tokens, (3 + j) * tokens)
        probs_ref[j : j + 1, :] = out[line : line + 1, part].astype(BF16)


def call(kernel, outs, *args, scalars=0, scratch=(), limit=32, far=0):
    size = sum(math.prod(a.shape) * a.dtype.itemsize for a in [*args, *outs])
    specs = [pl.BlockSpec(memory_space=pltpu.SMEM)] * scalars
    specs += [pl.BlockSpec(memory_space=pltpu.VMEM)] * (len(args) - scalars - far)
    specs += [pl.BlockSpec(memory_space=pl.ANY)] * far
    return pl.pallas_call(
        kernel,
        out_shape=outs,
        in_specs=specs,
        out_specs=[pl.BlockSpec(memory_space=pltpu.VMEM)] * len(outs),
        scratch_shapes=list(scratch),
        compiler_params=pltpu.CompilerParams(vmem_limit_bytes=limit * 1024 * 1024),
        cost_estimate=pl.CostEstimate(flops=0, bytes_accessed=size, transcendentals=0),
    )(*args)


def shape(dims, dtype=BF16):
    return jax.ShapeDtypeStruct(dims, dtype)


def shards(tokens, cotangent, routes, gate_probs, w_gate, w_up, w_down, tile_noise):
    nodes = lax.axis_size("node")
    local = lax.axis_size("local")
    chips = local // 2
    count, feats = tokens.shape
    slots = 2 * nodes
    gate, up, down, noise = w_gate[0], w_up[0], w_down[0], tile_noise[0]
    width, hid = gate.shape
    routes_t = routes.T
    same_core = [[2 * y + c for y in range(chips)] for c in range(2)]
    swap = [(i, i ^ 1) for i in range(local)]
    core = lax.rem(lax.axis_index("local"), 2).astype(jnp.int32).reshape(1)

    given = (routes_t, gate_probs.T, tokens.T, cotangent.T)
    (sent,) = call(
        pack_kernel,
        [pltpu.VMEM((8 * nodes, LANES), BF16)],
        *[held(a, pltpu.HBM) for a in given],
        scratch=[pltpu.VMEM(a.shape, a.dtype) for a in given] + [pltpu.SemaphoreType.DMA((4,))],
        far=4,
    )
    got = lax.all_to_all(sent.reshape(nodes, 8, LANES), "node", 0, 0, tiled=True)
    later, _ = lax.optimization_barrier((core, sent))
    scaled = call(
        scale_kernel,
        [
            pltpu.HBM((width, 2 * hid), BF16),
            pltpu.HBM((hid, width), BF16),
            pltpu.HBM((width, hid), BF16),
        ],
        later, gate, up, down, noise,
        scalars=1,
    )
    got, scaled = lax.optimization_barrier((got, scaled))
    tall, eff_down, down_t = scaled
    xdy, prob = call(
        unpack_kernel,
        [shape((2 * feats + TAIL, slots), F32), shape((8, slots), F32)],
        got.reshape(8 * nodes, LANES),
    )
    rows = lax.all_gather(xdy.astype(F16), "local", axis=0).astype(BF16)
    high = feats + 16
    keep, send, d_all = call(
        main_kernel,
        [
            pltpu.VMEM((chips, high, slots), BF16),
            pltpu.VMEM((chips, high, slots), BF16),
            pltpu.VMEM((slots, 3 * hid), BF16),
        ],
        core, prob, held(rows, pltpu.VMEM), *[held(a, pltpu.HBM) for a in (tall, eff_down)],
        scalars=1,
        scratch=[
            pltpu.VMEM((width, 2 * hid), BF16),
            pltpu.VMEM((hid, width), BF16),
            pltpu.VMEM((width, slots), BF16),
            pltpu.VMEM((width, slots), BF16),
            pltpu.SemaphoreType.DMA((2,)),
        ],
        far=2,
    )
    came = lax.ppermute(send, "local", swap)
    pair = (keep.astype(F32) + came.astype(F32)).astype(BF16)
    parts = lax.all_to_all(pair, "local", 0, 0, axis_index_groups=same_core, tiled=True)
    (noise_grad,) = call(
        noise_kernel,
        [shape(noise.shape, F32)],
        rows, d_all, gate, up, down_t,
        scratch=[pltpu.VMEM((width, slots), BF16), pltpu.VMEM((width, slots), BF16)],
    )
    (home,) = call(collect_kernel, [shape((4 * nodes, LANES))], parts)
    routes_later, home = lax.optimization_barrier((routes_t, home))
    back = lax.all_to_all(home.reshape(nodes, 4, LANES), "node", 0, 0, tiled=True)
    top = routes.shape[1]
    (chosen,) = call(choose_kernel, [shape((4 * nodes, (2 + top) * count))], routes_later)
    token_t, probs_t = call(
        finish_kernel,
        [shape((feats, count)), shape((top, count))],
        back.reshape(4 * nodes, LANES),
        chosen,
    )
    return token_t.T, probs_t.T, noise_grad[None]


def solution(mesh):
    in_specs = (
        P("node", "local"),
        P("node", "local"),
        P("node", None),
        P("node", None),
        P("node", None, "local"),
        P("node", None, "local"),
        P("node", "local", None),
        P("node", None, None, "local"),
    )
    out_specs = (P("node", "local"), P("node", None), P("node", None, None, "local"))
    return jax.shard_map(shards, mesh=mesh, in_specs=in_specs, out_specs=out_specs, check_vma=False)
```

```python
import math

import jax
import jax.numpy as jnp
from jax import lax
from jax.experimental import pallas as pl
from jax.experimental.pallas import tpu as pltpu
from jax.sharding import PartitionSpec as P

EXP_GROUP = 4
DEPTH = 16
NODE = ("x", "z")
LOCAL = ("y", "core")
LANES = 128
TAIL = 16
FACTORS = 3
held = pltpu.with_memory_space_constraint
F32 = jnp.float32
F16 = jnp.float16
BF16 = jnp.bfloat16
ROWS_BY_ROWS = (((0,), (0,)), ((), ()))
LANES_BY_LANES = (((1,), (1,)), ((), ()))


def dot(a, b, dims=(((1,), (0,)), ((), ()))):
    return lax.dot_general(a, b, dims, preferred_element_type=F32)


def select_rows(routes_ref, group, slot):
    top, tokens = routes_ref.shape
    first = group * EXP_GROUP
    matches = [routes_ref[j : j + 1, :] == first for j in range(top)]
    hit = jnp.zeros(group.shape, F32)
    for match in matches:
        hit = jnp.where(match, 1.0, hit)
    before = lax.broadcasted_iota(jnp.int32, (tokens, tokens), 0)
    after = lax.broadcasted_iota(jnp.int32, (tokens, tokens), 1)
    earlier = jnp.where(before < after, 1.0, 0.0).astype(BF16)
    rank = dot(hit.astype(BF16), earlier)
    return jnp.where(rank == slot.astype(F32), hit, 0.0), matches


def pack_kernel(
    routes_hbm, probs_hbm, x_hbm, dy_hbm, out_ref, routes_ref, probs_ref, x_ref, dy_ref, sems
):
    pairs = (
        (routes_hbm, routes_ref),
        (probs_hbm, probs_ref),
        (x_hbm, x_ref),
        (dy_hbm, dy_ref),
    )
    moves = [
        pltpu.make_async_copy(source, target, sems.at[i])
        for i, (source, target) in enumerate(pairs)
    ]
    for move in moves:
        move.start()
    rows, lanes = out_ref.shape
    for move in moves[:2]:
        move.wait()
    feats = x_ref.shape[0]
    row = lax.broadcasted_iota(jnp.int32, (rows, lanes), 0)
    block = lax.rem(row, 4)
    chosen, matches = select_rows(routes_ref, lax.div(row, 8), lax.rem(lax.div(row, 4), 2))
    weight = jnp.zeros(chosen.shape, F32)
    for j, match in enumerate(matches):
        weight = jnp.where(match, probs_ref[j : j + 1, :].astype(F32), weight)
    weight = jnp.sum(weight * chosen, axis=1, keepdims=True)
    for move in moves[2:]:
        move.wait()
    pad = jnp.zeros((4 * lanes - 2 * feats, lanes), BF16)
    both = jnp.concatenate([x_ref[...], dy_ref[...], pad], axis=0)
    picked = dot(chosen.astype(BF16), both, LANES_BY_LANES)
    out = jnp.zeros((rows, lanes), F32)
    for j in range(4):
        out = jnp.where(block == j, picked[:, j * lanes : (j + 1) * lanes], out)
    lane = lax.broadcasted_iota(jnp.int32, (rows, lanes), 1)
    out = jnp.where((block == 3) & (lane == 2 * feats - 3 * lanes), weight, out)
    out_ref[...] = out.astype(BF16)


def unpack_kernel(got_ref, xdy_ref, prob_ref):
    rows, lanes = got_ref.shape
    got = got_ref[...]
    row = lax.broadcasted_iota(jnp.int32, (rows, lanes), 0)
    col = lax.broadcasted_iota(jnp.int32, (rows, lanes), 1)
    parts = []
    for j in range(4):
        place = jnp.where(row == 4 * col + j, 1.0, 0.0).astype(BF16)
        parts.append(dot(got, place, ROWS_BY_ROWS))
    whole = jnp.concatenate(parts, axis=0)
    both = xdy_ref.shape[0] - TAIL
    feats = both // 2
    prob_ref[...] = whole[both : both + 8]
    undo = []
    for first in (0, feats):
        half = whole[first : first + feats]
        top = jnp.max(jnp.abs(half), axis=0, keepdims=True)
        raised = jnp.ones(top.shape, F32)
        for _ in range(FACTORS):
            factor = jnp.ones(top.shape, F32)
            for power in (256.0, 16.0, 4.0):
                fits = top * raised * power <= 32768.0
                raised = jnp.where(fits, raised * power, raised)
                factor = jnp.where(fits, factor / power, factor)
            undo.append(factor)
        xdy_ref[first : first + feats, :] = half * raised
    undo.append(jnp.ones((TAIL - 2 * FACTORS, lanes), F32))
    xdy_ref[both:, :] = jnp.concatenate(undo, axis=0)


def scale_kernel(
    after_ref, gate_ref, up_ref, down_ref, noise_ref, tall_ref, eff_down_ref, down_t_ref
):
    del after_ref
    blocks, lanes = noise_ref.shape[1:]
    for b in range(blocks):
        part = slice(b * lanes, (b + 1) * lanes)
        gate = gate_ref[part, :].astype(F32) * (1.0 + noise_ref[0, b : b + 1, :])
        up = up_ref[part, :].astype(F32) * (1.0 + noise_ref[1, b : b + 1, :])
        tall_ref[part, :lanes] = gate.astype(BF16)
        tall_ref[part, lanes:] = up.astype(BF16)
        down = down_ref[:, part].T
        down_t_ref[part, :] = down
        back = down.astype(F32) * (1.0 + noise_ref[2, b : b + 1, :])
        eff_down_ref[:, part] = back.astype(BF16).T


def lower(rows_ref, x_ref, dy_ref):
    feats = (rows_ref.shape[1] - TAIL) // 2
    for i in range(rows_ref.shape[0]):
        for j, target in enumerate((x_ref, dy_ref)):
            first = 2 * feats + j * FACTORS
            undo = jnp.ones((1, rows_ref.shape[2]), F32)
            for k in range(FACTORS):
                undo = undo * rows_ref[i, first + k : first + k + 1, :].astype(F32)
            value = rows_ref[i, j * feats : (j + 1) * feats, :].astype(F32) * undo
            target[i * feats : (i + 1) * feats, :] = value.astype(BF16)


def main_kernel(
    core_ref, prob_ref, rows_ref, tall_hbm, down_hbm,
    keep_ref, send_ref, d_ref, tall_ref, down_ref, x_ref, dy_ref, sems,
):
    width = tall_hbm.shape[0]
    pairs = ((tall_hbm, tall_ref.at[pl.ds(0, width)]), (down_hbm, down_ref))
    moves = [
        pltpu.make_async_copy(source, target, sems.at[i])
        for i, (source, target) in enumerate(pairs)
    ]
    for move in moves:
        move.start()
    lower(rows_ref, x_ref, dy_ref)
    core = core_ref[0]
    hid = down_ref.shape[0]
    moves[0].wait()
    pre = dot(x_ref[...], tall_ref[:width, :], ROWS_BY_ROWS).T
    moves[1].wait()
    back = dot(down_ref[...], dy_ref[...])
    pre_gate, pre_up = pre[:hid], pre[hid:]
    prob = prob_ref[0:1, :]
    sig = jax.nn.sigmoid(pre_gate)
    swish = pre_gate * sig
    hidden = (swish * pre_up).astype(BF16).astype(F32)
    grad_hidden = prob * back
    d_gate = grad_hidden * pre_up * sig * (1.0 + pre_gate * (1.0 - sig))
    d_up = grad_hidden * swish
    d_ref[:, :hid] = d_gate.T.astype(BF16)
    d_ref[:, hid : 2 * hid] = d_up.T.astype(BF16)
    d_ref[:, 2 * hid :] = (prob * hidden).T.astype(BF16)
    term = jnp.sum((hidden * back).T, axis=1, keepdims=True)
    columns, chips, rows, lanes = keep_ref.shape
    feats = x_ref.shape[0] // (2 * chips)
    lane = lax.broadcasted_iota(jnp.int32, (columns * rows, lanes), 1)
    last = jnp.where(lane == feats, term, 0.0)
    for chip in range(chips):
        for target, rank in ((send_ref, 1 - core), (keep_ref, core)):
            start = pl.multiple_of((2 * chip + rank) * feats, 32)
            value = dot(d_ref[:, : 2 * hid], tall_ref[pl.ds(start, lanes), :], LANES_BY_LANES)
            value = jnp.where(lane < feats, value, last).astype(BF16)
            for column in range(columns):
                target[column, chip] = value[column * rows : (column + 1) * rows]


def noise_kernel(rows_ref, d_ref, gate_ref, up_ref, down_t_ref, out_ref, x_ref, dy_ref):
    lower(rows_ref, x_ref, dy_ref)
    blocks, lanes = out_ref.shape[1:]
    for b in range(blocks):
        part = slice(b * lanes, (b + 1) * lanes)
        grad = dot(x_ref[part, :], d_ref[:, : 2 * lanes])
        grad_down = dot(dy_ref[part, :], d_ref[:, 2 * lanes :])
        pieces = (
            (gate_ref, grad[:, :lanes]),
            (up_ref, grad[:, lanes:]),
            (down_t_ref, grad_down),
        )
        for i, (weight, value) in enumerate(pieces):
            out_ref[i, b : b + 1, :] = jnp.sum(
                weight[part, :].astype(F32) * value, axis=0, keepdims=True
            )


def collect_kernel(parts_ref, out_ref):
    rows = out_ref.shape[0]
    depth = parts_ref.shape[1]
    columns = rows // depth
    chips = parts_ref.shape[0] // columns
    sums = []
    for column in range(columns):
        total = parts_ref[column * chips].astype(F32)
        for chip in range(1, chips):
            total = total + parts_ref[column * chips + chip].astype(F32)
        sums.append(total.astype(BF16))
    row = lax.broadcasted_iota(jnp.int32, (rows, rows), 0)
    col = lax.broadcasted_iota(jnp.int32, (rows, rows), 1)
    source = lax.rem(lax.div(row, 2), columns) * depth
    source = source + 2 * lax.div(row, 2 * columns) + lax.rem(row, 2)
    place = jnp.where(col == source, 1.0, 0.0).astype(BF16)
    out_ref[...] = dot(place, jnp.concatenate(sums, axis=0)).astype(BF16)


def choose_kernel(routes_ref, out_ref):
    rows = out_ref.shape[0]
    tokens = routes_ref.shape[1]
    columns = rows // (2 * DEPTH)
    row = lax.broadcasted_iota(jnp.int32, (rows, tokens), 0)
    group = lax.rem(lax.div(row, 2), columns) * DEPTH + lax.div(row, 2 * columns)
    chosen, matches = select_rows(routes_ref, group, lax.rem(row, 2))
    masks = [chosen] + [jnp.where(match, chosen, 0.0) for match in matches]
    for i, mask in enumerate(masks):
        out_ref[:, i * tokens : (i + 1) * tokens] = mask.astype(BF16)


def finish_kernel(back_ref, chosen_ref, tokens_ref, probs_ref):
    feats, tokens = tokens_ref.shape
    out = dot(back_ref[...], chosen_ref[...], ROWS_BY_ROWS)
    tokens_ref[...] = out[:feats, :tokens].astype(BF16)
    for j in range(probs_ref.shape[0]):
        part = slice((1 + j) * tokens, (2 + j) * tokens)
        probs_ref[j : j + 1, :] = out[feats : feats + 1, part].astype(BF16)


def call(kernel, outs, *args, scalars=0, scratch=(), limit=32, far=0):
    size = sum(math.prod(a.shape) * a.dtype.itemsize for a in [*args, *outs])
    specs = [pl.BlockSpec(memory_space=pltpu.SMEM)] * scalars
    specs += [pl.BlockSpec(memory_space=pltpu.VMEM)] * (len(args) - scalars - far)
    specs += [pl.BlockSpec(memory_space=pl.ANY)] * far
    return pl.pallas_call(
        kernel,
        out_shape=outs,
        in_specs=specs,
        out_specs=[pl.BlockSpec(memory_space=pltpu.VMEM)] * len(outs),
        scratch_shapes=list(scratch),
        compiler_params=pltpu.CompilerParams(vmem_limit_bytes=limit * 1024 * 1024),
        cost_estimate=pl.CostEstimate(flops=0, bytes_accessed=size, transcendentals=0),
    )(*args)


def shape(dims, dtype=BF16):
    return jax.ShapeDtypeStruct(dims, dtype)


def shards(tokens, cotangent, routes, gate_probs, w_gate, w_up, w_down, tile_noise):
    columns = lax.axis_size("x")
    nodes = columns * lax.axis_size("z")
    chips = lax.axis_size("y")
    count, feats = tokens.shape
    slots = 2 * nodes
    gate, up, down, noise = w_gate[0], w_up[0], w_down[0], tile_noise[0]
    width, hid = gate.shape
    routes_t = routes.T
    swap = [(0, 1), (1, 0)]
    core = lax.axis_index("core").astype(jnp.int32).reshape(1)

    given = (routes_t, gate_probs.T, tokens.T, cotangent.T)
    (sent,) = call(
        pack_kernel,
        [pltpu.VMEM((8 * nodes, LANES), BF16)],
        *[held(a, pltpu.HBM) for a in given],
        scratch=[pltpu.VMEM(a.shape, a.dtype) for a in given] + [pltpu.SemaphoreType.DMA((4,))],
        far=4,
    )
    got = lax.all_to_all(sent.reshape(nodes, 8, LANES), NODE, 0, 0, tiled=True)
    later, _ = lax.optimization_barrier((core, sent))
    scaled = call(
        scale_kernel,
        [
            pltpu.HBM((width, 2 * hid), BF16),
            pltpu.HBM((hid, width), BF16),
            pltpu.HBM((width, hid), BF16),
        ],
        later, gate, up, down, noise,
        scalars=1,
    )
    got, scaled = lax.optimization_barrier((got, scaled))
    tall, eff_down, down_t = scaled
    xdy, prob = call(
        unpack_kernel,
        [shape((2 * feats + TAIL, slots), F32), shape((8, slots), F32)],
        got.reshape(8 * nodes, LANES),
    )
    rows = lax.all_gather(xdy.astype(F16), LOCAL, axis=0).astype(BF16)
    lanes = 2 * LANES
    height = slots // columns
    keep, send, d_all = call(
        main_kernel,
        [
            pltpu.VMEM((columns, chips, height, lanes), BF16),
            pltpu.VMEM((columns, chips, height, lanes), BF16),
            pltpu.VMEM((slots, 3 * hid), BF16),
        ],
        core, prob, held(rows, pltpu.VMEM), *[held(a, pltpu.HBM) for a in (tall, eff_down)],
        scalars=1,
        scratch=[
            pltpu.VMEM((width + lanes - feats, 2 * hid), BF16),
            pltpu.VMEM((hid, width), BF16),
            pltpu.VMEM((width, slots), BF16),
            pltpu.VMEM((width, slots), BF16),
            pltpu.SemaphoreType.DMA((2,)),
        ],
        far=2,
    )
    came = lax.ppermute(send, "core", swap)
    pair = (keep.astype(F32) + came.astype(F32)).astype(BF16)
    pair = pair.reshape(columns * chips, height, lanes)
    parts = lax.all_to_all(pair, ("x", "y"), 0, 0, tiled=True)
    (noise_grad,) = call(
        noise_kernel,
        [shape(noise.shape, F32)],
        rows, d_all, gate, up, down_t,
        scratch=[pltpu.VMEM((width, slots), BF16), pltpu.VMEM((width, slots), BF16)],
    )
    (home,) = call(collect_kernel, [shape((slots, lanes))], parts)
    routes_later, home = lax.optimization_barrier((routes_t, home))
    home = home.reshape(DEPTH, 2 * columns, lanes)
    back = lax.all_to_all(home, "z", 0, 0, tiled=True).reshape(slots, lanes)
    top = routes.shape[1]
    (chosen,) = call(choose_kernel, [shape((slots, (1 + top) * count))], routes_later)
    token_t, probs_t = call(
        finish_kernel, [shape((feats, count)), shape((top, count))], back, chosen
    )
    return token_t.T, probs_t.T, noise_grad[None]


def solution(mesh):
    nodes, local = mesh.devices.shape
    devices = mesh.devices.reshape(nodes // DEPTH, DEPTH, local // 2, 2)
    in_specs = (
        P(NODE, LOCAL),
        P(NODE, LOCAL),
        P(NODE, None),
        P(NODE, None),
        P(NODE, None, LOCAL),
        P(NODE, None, LOCAL),
        P(NODE, LOCAL, None),
        P(NODE, None, None, LOCAL),
    )
    out_specs = (P(NODE, LOCAL), P(NODE, None), P(NODE, None, None, LOCAL))
    return jax.shard_map(
        shards,
        mesh=jax.sharding.Mesh(devices, NODE + LOCAL),
        in_specs=in_specs,
        out_specs=out_specs,
        check_vma=False,
    )
```
